512 devices in a mesh: resp: 64 (over z, y_hi, x), head: 8 (over y_lo, core).
Axes of the slice: x: 4, y: 8 (y_hi: 2, y_lo: 4; y = y_hi * 4 + y_lo), z: 8, core: 2. Of those that a mesh axis runs over, the one named last changes fastest.
Arguments:
- ssm_input: bfloat16 [32768, 8192], P('resp', 'head'), may hold values from -6 to 6
- b_proj: bfloat16 [32768, 1024], P('resp', 'head'), may hold values from -0.5 to 0.5
- c_proj: bfloat16 [32768, 1024], P('resp', 'head'), may hold values from -6 to 6
- step_size: float32 [32768, 128], P('resp', 'head'), may hold values from 0.02 to 0.2
- a_log: float32 [128], P('head'), may hold values from -3 to 1.5
- d_skip: float32 [128], P('head'), may hold values from 0.5 to 1.5
- out_weight: bfloat16 [8192, 2048], P(('head', 'resp')), may hold values from -0.0625 to 0.0625
- prompt_state: bfloat16 [64, 128, 64, 128], P('resp', 'head'), may hold values from -0.59765625 to 0.59765625
- prompt_of: int32 [512], P('resp'), may hold values from 0 to 63, as said below
- out_grad: bfloat16 [32768, 2048], P(('resp', 'head')), may hold values from -6 to 6
Outputs:
- layer_out: bfloat16 [32768, 2048], P(('resp', 'head'))
- grad_input: bfloat16 [32768, 8192], P('resp', 'head')
- grad_state: float32 [64, 128, 64, 128], P('resp', 'head')
The draws below stay inside these ranges and needn't reach their ends.
Inputs may be any that keep to these rules, and one draw needn't show every extreme that they name: `prompt_of`: for every g, responses 8 * 8 * g to 8 * 8 * (g + 1) - 1 name only prompts 8 * g to 8 * (g + 1) - 1, and every prompt is named by exactly 8 responses.
All inputs are finite; a program needn't handle non-finite values.
Results may differ from the reference program's by a relative error of at most 0.0051.
Values may be sent and summed in bfloat16 or wider, within the bound.
A program may use at most 64 MiB of HBM per device.

```python
import math
import jax
import jax.numpy as jnp
from jax import lax

H = 128
P_SIZE = 64
NS = 128
GROUPS = 8
DW = 2048
SPAN = 64
FAN = 8
R_DEV = 8
RESPONSES = 512
PROMPTS = 64
TOKENS = 32768
INNER = 8192


def draw_prompt_of(key, part):
    key = jax.random.fold_in(key, 11)
    block_size = R_DEV * FAN
    group_count = RESPONSES // block_size
    group_keys = jax.random.split(key, group_count)

    def shuffle(subkey):
        return jax.random.permutation(subkey, block_size)
    orders = jax.vmap(shuffle)(group_keys).astype(jnp.int32)
    firsts = jnp.arange(group_count, dtype=jnp.int32)[:, None] * R_DEV
    return (firsts + orders // FAN).reshape(RESPONSES).astype(jnp.int32)


def shard_levels(own_key, shape, cuts, smallest, top_value):
    gain = 1.0
    for position, parts in cuts:
        draws = jax.random.uniform(jax.random.fold_in(jax.random.fold_in(own_key, 6), position), (parts,), jnp.float32, smallest / len(cuts), top_value / len(cuts))
        gain = gain * jnp.repeat(jnp.exp(draws), shape[position] // parts).reshape((-1,) + (1,) * (len(shape) - 1 - position))
    return gain


def scatter_about(own_key, dims, deviation, bound, cuts=(), held_as=jnp.bfloat16):
    loudness = shard_levels(own_key, dims, cuts, -0.22, 0.18) if cuts else 1.0
    values = jax.random.normal(own_key, dims, jnp.float32) * deviation * loudness
    return jnp.minimum(jnp.maximum(values, -bound), bound).astype(held_as)


def setup_inputs(seed: int = 0) -> dict:
    streams_of = jax.random.split(jax.random.key(seed), 11)
    return {
        "ssm_input": scatter_about(streams_of[0], (TOKENS, INNER), 1.0, 6.0, ((0, 64), (1, 8))),
        "b_proj": scatter_about(streams_of[1], (TOKENS, GROUPS * NS), NS ** -0.5, 0.5, ((0, 64), (1, 8))),
        "c_proj": scatter_about(streams_of[2], (TOKENS, GROUPS * NS), 1.0, 6.0, ((0, 64), (1, 8))),
        "step_size": jnp.clip(jnp.exp(math.log(0.2) - 2.3025851 * jax.random.uniform(streams_of[3], (TOKENS, H), jnp.float32) ** shard_levels(streams_of[3], (TOKENS, H), ((0, 64), (1, 8)), -0.2, 0.2)), 0.02, 0.2),
        "a_log": jnp.clip(-3.0 + 4.5 * jax.random.uniform(streams_of[4], (H,), jnp.float32) ** shard_levels(streams_of[4], (H,), ((0, 8),), -0.2, 0.2), -3.0, 1.5),
        "d_skip": jnp.clip(0.5 + 1.0 * jax.random.uniform(streams_of[5], (H,), jnp.float32) ** shard_levels(streams_of[5], (H,), ((0, 8),), -0.2, 0.2), 0.5, 1.5),
        "out_weight": scatter_about(streams_of[6], (INNER, DW), INNER ** -0.5, 0.0625, ((0, 512),)),
        "prompt_state": scatter_about(streams_of[7], (PROMPTS, H, P_SIZE, NS), 0.1, 0.59765625, ((0, 64), (1, 8))),
        "prompt_of": draw_prompt_of(jax.random.fold_in(streams_of[10], 71), 0),
        "out_grad": scatter_about(streams_of[9], (TOKENS, DW), 1.0, 6.0, ((0, 512),)),
    }


def span_terms(x_rows, b_rows, c_rows, step_rows, a_negative, d_skip):
    per_group = H // GROUPS
    x_blocks = x_rows.reshape(SPAN, GROUPS, per_group, P_SIZE).astype(jnp.float32)
    b_blocks = b_rows.reshape(SPAN, GROUPS, NS).astype(jnp.float32)
    c_blocks = c_rows.reshape(SPAN, GROUPS, NS).astype(jnp.float32)
    scores = jnp.einsum("tgn,sgn->gts", c_blocks, b_blocks)
    cumulative = jnp.cumsum(step_rows * a_negative[None, :], axis=0).reshape(SPAN, GROUPS, per_group)
    cum_heads = jnp.transpose(cumulative, (1, 2, 0))
    causal = jnp.arange(SPAN)[:, None] >= jnp.arange(SPAN)[None, :]
    differ = cum_heads[:, :, :, None] - cum_heads[:, :, None, :]
    decays = jnp.where(causal, jnp.exp(jnp.where(causal, differ, 0.0)), 0.0)
    step_heads = jnp.transpose(step_rows.reshape(SPAN, GROUPS, per_group), (1, 2, 0))
    mixing = (decays * step_heads[:, :, None, :] * scores[:, None, :, :]).astype(jnp.bfloat16)
    mixing = lax.optimization_barrier(mixing).astype(jnp.float32)
    growth = jnp.exp(cumulative)
    skip_gain = d_skip.reshape(GROUPS, per_group)[None, :, :, None]
    return x_blocks, c_blocks, mixing, growth, skip_gain


def forward_rows(x_rows, b_rows, c_rows, step_rows, a_negative, d_skip, initial):
    per_group = H // GROUPS
    x_blocks, c_blocks, mixing, growth, skip_gain = span_terms(x_rows, b_rows, c_rows, step_rows, a_negative, d_skip)
    within = jnp.einsum("ghts,sghp->tghp", mixing, x_blocks)
    init_blocks = initial.reshape(GROUPS, per_group, P_SIZE, NS).astype(jnp.float32)
    carried = jnp.einsum("ghpn,tgn->tghp", init_blocks, c_blocks) * growth[:, :, :, None]
    return (carried + within + skip_gain * x_blocks).astype(jnp.bfloat16).reshape(SPAN, H * P_SIZE)


def backward_rows(x_rows, b_rows, c_rows, step_rows, a_negative, d_skip, back_rows):
    per_group = H // GROUPS
    x_blocks, c_blocks, mixing, growth, skip_gain = span_terms(x_rows, b_rows, c_rows, step_rows, a_negative, d_skip)
    back_blocks = back_rows.reshape(SPAN, GROUPS, per_group, P_SIZE).astype(jnp.float32)
    grad_rows = jnp.einsum("ghts,tghp->sghp", mixing, back_blocks) + skip_gain * back_blocks
    scaled = (growth[:, :, :, None] * back_blocks).astype(jnp.bfloat16)
    scaled = lax.optimization_barrier(scaled).astype(jnp.float32)
    grad_init = jnp.einsum("tghp,tgn->ghpn", scaled, c_blocks).reshape(H, P_SIZE, NS)
    return grad_rows.astype(jnp.bfloat16).reshape(SPAN, H * P_SIZE), grad_init


def reference(ssm_input, b_proj, c_proj, step_size, a_log, d_skip, out_weight, prompt_state, prompt_of, out_grad):
    a_negative = -jnp.exp(a_log)
    responses = prompt_of.shape[0]
    x_all = ssm_input.reshape(responses, SPAN, H * P_SIZE)
    b_all = b_proj.reshape(responses, SPAN, GROUPS * NS)
    c_all = c_proj.reshape(responses, SPAN, GROUPS * NS)
    step_all = step_size.reshape(responses, SPAN, H)

    def forward_one(packed):
        x_rows, b_rows, c_rows, step_rows, prompt = packed
        initial = lax.dynamic_index_in_dim(prompt_state, prompt, 0, keepdims=False)
        return forward_rows(x_rows, b_rows, c_rows, step_rows, a_negative, d_skip, initial)

    ssm_out = lax.map(forward_one, (x_all, b_all, c_all, step_all, prompt_of)).reshape(-1, H * P_SIZE)
    layer_out = jnp.dot(ssm_out, out_weight, preferred_element_type=jnp.float32).astype(jnp.bfloat16)
    back_grad = jnp.dot(out_grad, out_weight.T, preferred_element_type=jnp.float32).astype(jnp.bfloat16)
    back_all = back_grad.reshape(responses, SPAN, H * P_SIZE)

    def backward_one(running, packed):
        x_rows, b_rows, c_rows, step_rows, back_rows, prompt = packed
        grad_rows, grad_init = backward_rows(x_rows, b_rows, c_rows, step_rows, a_negative, d_skip, back_rows)
        current = lax.dynamic_index_in_dim(running, prompt, 0, keepdims=False)
        running = lax.dynamic_update_index_in_dim(running, current + grad_init, prompt, 0)
        return running, grad_rows

    zero_state = jnp.zeros(prompt_state.shape, jnp.float32)
    grad_state, grad_rows = lax.scan(backward_one, zero_state, (x_all, b_all, c_all, step_all, back_all, prompt_of))
    return layer_out, grad_rows.reshape(-1, H * P_SIZE), grad_state
```

```python
import functools

import jax
import jax.numpy as jnp
from jax import lax
from jax.experimental import pallas as pl
from jax.experimental.pallas import tpu as pltpu
from jax.sharding import PartitionSpec as P

MESH = pl.DeviceIdType.MESH
F32 = jnp.float32
BF16 = jnp.bfloat16
HIGHEST = lax.Precision.HIGHEST

NX, NYH, NZ, NYL, NCORE = 4, 2, 8, 4, 2
GROUP = NX * NYH
RESP_ROWS = 64
RESPS = 8
ROWS = RESP_ROWS * RESPS
NS = 128
HEADS = 16
WIDTH = 1024
DW = 2048
SHARD = 16
LANE = 128
PAIRS = WIDTH // LANE
NBLK = 4
BLK = DW // NBLK


def dot_nt(a, b):
    return lax.dot_general(a, b, (((1,), (1,)), ((), ())), preferred_element_type=F32)


def dot_tn(a, b):
    return lax.dot_general(a, b, (((0,), (0,)), ((), ())), preferred_element_type=F32)


def chunk_of(z, s):
    far = (s + 1) // 2
    sign = 1 - 2 * (s % 2)
    return lax.rem(z + NZ + sign * far, NZ)


def kernel(
    prompt_ref,
    x_ref,
    b_ref,
    c_ref,
    step_ref,
    alog_ref,
    skip_ref,
    w_ref,
    state_ref,
    og_ref,
    layer_ref,
    gin_ref,
    gstate_ref,
    w_all,
    og_all,
    states,
    csel,
    mix,
    mix_t,
    growth,
    ssm,
    back,
    p_tmp,
    p_send,
    p_recv,
    r_own,
    r_send,
    r_recv,
    g_tmp,
    g_own,
    g_send,
    g_recv,
    gy_send,
    gy_recv,
    loc_sem,
    wy_s,
    wy_r,
    wx_s,
    wx_r,
    wz_s,
    wz_r,
    sy_s,
    sy_r,
    sx_s,
    sx_r,
    sf_s,
    sf_r,
    oy_s,
    oy_r,
    oc_s,
    oc_r,
    gx_s,
    gx_r,
    gy_s,
    gy_r,
    pp_s,
    pp_r,
    rr_s,
    rr_r,
):
    resp = lax.axis_index("resp")
    head = lax.axis_index("head")
    x = lax.rem(resp, NX)
    yh = lax.rem(resp // NX, NYH)
    z = resp // GROUP
    core = lax.rem(head, NCORE)
    yl = head // NCORE

    def resp_at(z_, yh_, x_):
        return z_ * GROUP + yh_ * NX + x_

    def dev_x(j):
        return (resp_at(z, yh, lax.rem(x + NX + j, NX)), head)

    def dev_z(j):
        return (resp_at(lax.rem(z + NZ + j, NZ), yh, x), head)

    dev_yh = (resp_at(z, 1 - yh, x), head)
    dev_core = (resp, yl * NCORE + 1 - core)

    def dev_yl(j):
        return (resp, lax.rem(yl + NYL + j, NYL) * NCORE + core)

    def send(src, dst, ss, rs, dev):
        copy = pltpu.make_async_remote_copy(
            src_ref=src, dst_ref=dst, send_sem=ss, recv_sem=rs, device_id=dev, device_id_type=MESH
        )
        copy.start()
        return copy

    def landed(dst, ss, rs, dev):
        pltpu.make_async_remote_copy(
            src_ref=dst, dst_ref=dst, send_sem=ss, recv_sem=rs, device_id=dev, device_id_type=MESH
        ).wait_recv()

    pending = []

    barrier = pltpu.get_barrier_semaphore()
    partners = [dev_yh, dev_core, dev_z(1), dev_z(-1)]
    partners += [dev_x(j) for j in (1, 2, 3)] + [dev_yl(j) for j in (1, 2, 3)]
    for dev in partners:
        pl.semaphore_signal(barrier, inc=1, device_id=dev, device_id_type=MESH)
    pl.semaphore_wait(barrier, len(partners))

    def w_rows(z_, yh_, x_):
        return w_all.at[pl.ds(pl.multiple_of(resp_at(z_, yh_, x_) * SHARD, SHARD), SHARD), :]

    def w_half(z_, yh_):
        start = (z_ * NYH + yh_) * (NX * SHARD)
        return w_all.at[pl.ds(pl.multiple_of(start, NX * SHARD), NX * SHARD), :]

    pending.append(send(w_ref, w_rows(z, yh, x), wy_s, wy_r, dev_yh))
    for j in (1, 2, 3):
        pending.append(
            send(w_ref, w_rows(z, yh, x), wx_s.at[0, j - 1], wx_r.at[0, j - 1], dev_x(j))
        )
    my_slot = yh * NX + x
    og_rows = lambda h_: og_all.at[pl.ds(pl.multiple_of(h_ * RESP_ROWS, RESP_ROWS), RESP_ROWS), :]
    local = [
        pltpu.make_async_copy(w_ref, w_rows(z, yh, x), loc_sem.at[0]),
        pltpu.make_async_copy(state_ref, states.at[my_slot], loc_sem.at[1]),
        pltpu.make_async_copy(og_ref, og_rows(head), loc_sem.at[2]),
    ]
    for copy in local:
        copy.start()

    base = (resp // GROUP) * GROUP

    def fill_csel(r, carry):
        rows = pl.ds(pl.multiple_of(r * RESP_ROWS, RESP_ROWS), RESP_ROWS)
        slot = prompt_ref[r] - base
        c_rows = c_ref[rows, :].astype(F32)
        for k in range(GROUP):
            keep = jnp.where(slot == k, 1.0, 0.0).astype(F32)
            csel[rows, k * NS : (k + 1) * NS] = (c_rows * keep).astype(BF16)
        return carry

    lax.fori_loop(0, RESPS, fill_csel, 0)

    row_id = lax.broadcasted_iota(jnp.int32, (RESP_ROWS, LANE), 0)
    lane_id = lax.broadcasted_iota(jnp.int32, (RESP_ROWS, LANE), 1)
    lane_pos = lax.rem(lane_id, RESP_ROWS)
    first = lane_id < RESP_ROWS
    diag = lane_pos == row_id
    earlier = lane_pos <= row_id
    later = lane_pos >= row_id
    tri = (
        lax.broadcasted_iota(jnp.int32, (RESP_ROWS, RESP_ROWS), 0)
        >= lax.broadcasted_iota(jnp.int32, (RESP_ROWS, RESP_ROWS), 1)
    ).astype(F32)
    a_neg = -jnp.exp(alog_ref[...])

    def spread(columns, i):
        return jnp.where(first, columns[:, 2 * i : 2 * i + 1], columns[:, 2 * i + 1 : 2 * i + 2])

    def fill_mix(r, carry):
        rows = pl.ds(pl.multiple_of(r * RESP_ROWS, RESP_ROWS), RESP_ROWS)
        c_rows, b_rows = c_ref[rows, :], b_ref[rows, :]
        steps = step_ref[rows, :]
        cum = lax.dot_general(
            tri, steps * a_neg, (((1,), (0,)), ((), ())),
            precision=HIGHEST, preferred_element_type=F32,
        )
        score = dot_nt(c_rows, jnp.concatenate([b_rows, b_rows], axis=0))
        score_t = dot_nt(b_rows, jnp.concatenate([c_rows, c_rows], axis=0))
        for i in range(PAIRS):
            cols = slice(i * LANE, (i + 1) * LANE)
            cum_i, step_i = spread(cum, i), spread(steps, i)
            cum_row = jnp.sum(jnp.where(diag, cum_i, 0.0), axis=0, keepdims=True)
            step_row = jnp.sum(jnp.where(diag, step_i, 0.0), axis=0, keepdims=True)
            differ = cum_i - cum_row
            decay = jnp.exp(jnp.where(earlier, differ, 0.0))
            mix[rows, cols] = jnp.where(earlier, decay * step_row * score, 0.0).astype(BF16)
            decay_t = jnp.exp(jnp.where(later, -differ, 0.0))
            mix_t[rows, cols] = jnp.where(later, decay_t * step_i * score_t, 0.0).astype(BF16)
            growth[rows, cols] = jnp.exp(cum_i)
        return carry

    block_mask = (
        (lax.broadcasted_iota(jnp.int32, (LANE, LANE), 0) < RESP_ROWS)
        == (lax.broadcasted_iota(jnp.int32, (LANE, LANE), 1) < RESP_ROWS)
    ).astype(F32).astype(BF16)

    def blocks_of(pair):
        return jnp.concatenate([pair, pair], axis=0) * block_mask

    landed(w_rows(z, 1 - yh, x), wy_s, wy_r, dev_yh)
    for j in (1, 2, 3):
        piece = w_rows(z, 1 - yh, x)
        pending.append(send(piece, piece, wx_s.at[1, j - 1], wx_r.at[1, j - 1], dev_x(j)))
    pending.append(send(state_ref, states.at[my_slot], sy_s, sy_r, dev_yh))
    for i, j in enumerate((1, -1)):
        pending.append(
            send(state_ref, states.at[my_slot], sx_s.at[0, i], sx_r.at[0, i], dev_x(j))
        )
    pending.append(send(og_ref, og_rows(head), oc_s.at[0], oc_r.at[0], dev_core))
    for j in (1, 2, 3):
        pending.append(send(og_ref, og_rows(head), oy_s.at[j - 1], oy_r.at[j - 1], dev_yl(j)))

    local[0].wait()
    for j in (1, 2, 3):
        landed(w_rows(z, yh, lax.rem(x + NX - j, NX)), wx_s.at[0, j - 1], wx_r.at[0, j - 1], dev_x(-j))

    def send_z(step, half):
        yh_ = yh if half == 0 else 1 - yh
        for d, sign in enumerate((1, -1)):
            if step == 3 and half != d:
                continue
            piece = w_half(lax.rem(z + NZ - sign * step, NZ), yh_)
            pending.append(
                send(piece, piece, wz_s.at[d, step, half], wz_r.at[d, step, half], dev_z(sign))
            )

    def land_z(step, half):
        yh_ = yh if half == 0 else 1 - yh
        for d, sign in enumerate((1, -1)):
            if step == 3 and half != d:
                continue
            piece = w_half(lax.rem(z + NZ - sign * (step + 1), NZ), yh_)
            landed(piece, wz_s.at[d, step, half], wz_r.at[d, step, half], dev_z(-sign))

    send_z(0, 0)
    for j in (1, 2, 3):
        landed(
            w_rows(z, 1 - yh, lax.rem(x + NX - j, NX)),
            wx_s.at[1, j - 1],
            wx_r.at[1, j - 1],
            dev_x(-j),
        )
    send_z(0, 1)

    lax.fori_loop(0, 4, fill_mix, 0)

    def slot_of(yh_, j):
        return yh_ * NX + lax.rem(x + NX + j, NX)

    landed(states.at[slot_of(1 - yh, 0)], sy_s, sy_r, dev_yh)
    for i, j in enumerate((1, -1)):
        piece = states.at[slot_of(1 - yh, 0)]
        pending.append(send(piece, piece, sx_s.at[1, i], sx_r.at[1, i], dev_x(j)))

    def pass_states(n, yh_):
        for i, j in enumerate((1, -1)):
            landed(states.at[slot_of(yh_, -j)], sx_s.at[n, i], sx_r.at[n, i], dev_x(-j))
            piece = states.at[slot_of(yh_, -j), pl.ds(i * (WIDTH // 2), WIDTH // 2), :]
            pending.append(send(piece, piece, sf_s.at[n, i], sf_r.at[n, i], dev_x(j)))

    pass_states(0, yh)
    lax.fori_loop(4, RESPS, fill_mix, 0)

    for half in (0, 1):
        land_z(0, half)
        send_z(1, half)

    pass_states(1, 1 - yh)

    local[2].wait()
    landed(og_rows(yl * NCORE + 1 - core), oc_s.at[0], oc_r.at[0], dev_core)
    for j in (1, 2, 3):
        piece = og_rows(lax.rem(yl + NYL - j, NYL) * NCORE + core)
        landed(piece, oy_s.at[j - 1], oy_r.at[j - 1], dev_yl(-j))
        pending.append(send(piece, piece, oc_s.at[j], oc_r.at[j], dev_core))

    local[1].wait()
    for n, yh_ in enumerate((yh, 1 - yh)):
        for i, j in enumerate((1, -1)):
            piece = states.at[slot_of(yh_, 2), pl.ds(i * (WIDTH // 2), WIDTH // 2), :]
            landed(piece, sf_s.at[n, i], sf_r.at[n, i], dev_x(-j))

    for half in (0, 1):
        land_z(1, half)
        send_z(2, half)

    def spread_row(row_ref, i):
        row = row_ref[...]
        where_first = lax.broadcasted_iota(jnp.int32, (1, LANE), 1) < RESP_ROWS
        out = jnp.zeros((1, LANE), F32)
        for h in range(HEADS):
            keep = jnp.where(h // 2 == i, 1.0, 0.0).astype(F32)
            mine = where_first if h % 2 == 0 else jnp.logical_not(where_first)
            out = out + jnp.where(mine, row[:, h : h + 1] * keep, 0.0)
        return out

    def forward(i, carry):
        cols = pl.ds(pl.multiple_of(i * LANE, LANE), LANE)
        skip = spread_row(skip_ref, i)
        init = jnp.concatenate([states[k, cols, :] for k in range(GROUP)], axis=1)
        carried = dot_nt(csel[...], init) * growth[:, cols]
        for r in range(RESPS):
            rows = slice(r * RESP_ROWS, (r + 1) * RESP_ROWS)
            x_rows = x_ref[rows, cols]
            within = jnp.dot(
                mix[rows, cols], blocks_of(x_rows), preferred_element_type=F32
            )
            ssm[rows, cols] = (carried[rows, :] + within + skip * x_rows.astype(F32)).astype(BF16)
        return carry

    lax.fori_loop(0, PAIRS, forward, 0)

    for j in (1, 2, 3):
        piece = og_rows(lax.rem(yl + NYL - j, NYL) * NCORE + 1 - core)
        landed(piece, oc_s.at[j], oc_r.at[j], dev_core)

    def g_piece(ref, j, s):
        return ref.at[j - 1, s]

    def backward(s, carry):
        start = chunk_of(z, s) * LANE
        span = pl.ds(pl.multiple_of(start, LANE), LANE)
        back_f = dot_nt(og_all[...], w_all[span, :])
        back_b = back_f.astype(BF16)
        back[:, span] = back_b
        scaled = (growth[:, span] * back_b.astype(F32)).astype(BF16)
        g_tmp[...] = dot_tn(scaled, csel[...])
        for j in range(NX):
            for y in range(NYH):
                k = y * NX + lax.rem(x + j, NX)
                part = g_tmp[:, pl.ds(pl.multiple_of(k * NS, NS), NS)]
                if j == 0:
                    g_own[s, y] = part
                else:
                    g_send[j - 1, s, y] = part.astype(BF16)
            if j > 0:
                send(
                    g_piece(g_send, j, s), g_piece(g_recv, j, s),
                    gx_s.at[j - 1, s], gx_r.at[j - 1, s], dev_x(j),
                )
        return carry

    def add_x(s, carry):
        for j in (1, 2, 3):
            landed(g_piece(g_recv, j, s), gx_s.at[j - 1, s], gx_r.at[j - 1, s], dev_x(-j))
        span = pl.ds(pl.multiple_of(chunk_of(z, s) * LANE, LANE), LANE)

        def total(y):
            return g_own[s, y] + (
                g_recv[0, s, y].astype(F32) + g_recv[1, s, y].astype(F32) + g_recv[2, s, y].astype(F32)
            )

        gy_send[s] = total(1 - yh).astype(BF16)
        send(gy_send.at[s], gy_recv.at[s], gy_s.at[s], gy_r.at[s], dev_yh)
        gstate_ref[span, :] = total(yh)
        return carry

    lax.fori_loop(0, 3, backward, 0)
    for half in (0, 1):
        land_z(2, half)
        send_z(3, half)
    lax.fori_loop(3, 5, backward, 0)
    lax.fori_loop(0, 3, add_x, 0)
    lax.fori_loop(5, 7, backward, 0)
    for half in (0, 1):
        land_z(3, half)

    def project(n, carry):
        cols = pl.ds(pl.multiple_of(n * BLK, BLK), BLK)
        p_tmp[...] = jnp.dot(ssm[...], w_all[:, cols], preferred_element_type=F32)
        for j in range(NYL):
            other = (lax.rem(yl + j, NYL) * NCORE + 1 - core) * RESP_ROWS
            mine = (lax.rem(yl + j, NYL) * NCORE + core) * RESP_ROWS
            dst_row = lax.rem(yl + j, NYL)
            p_send[n, dst_row] = p_tmp[
                pl.ds(pl.multiple_of(other, RESP_ROWS), RESP_ROWS), :
            ].astype(BF16)
            r_own[n, j] = p_tmp[pl.ds(pl.multiple_of(mine, RESP_ROWS), RESP_ROWS), :]
        send(p_send.at[n], p_recv.at[n], pp_s.at[n], pp_r.at[n], dev_core)
        return carry

    def share(n, carry):
        landed(p_recv.at[n], pp_s.at[n], pp_r.at[n], dev_core)
        for j in range(NYL):
            total = r_own[n, j] + p_recv[n, lax.rem(yl + j, NYL)].astype(F32)
            if j == 0:
                r_own[n, 0] = total
            else:
                r_send[j - 1, n] = total.astype(BF16)
                send(
                    r_send.at[j - 1, n], r_recv.at[j - 1, n],
                    rr_s.at[j - 1, n], rr_r.at[j - 1, n], dev_yl(j),
                )
        return carry

    lax.fori_loop(0, NBLK, project, 0)
    lax.fori_loop(0, NBLK, share, 0)
    lax.fori_loop(7, 8, backward, 0)
    lax.fori_loop(3, 8, add_x, 0)

    def input_grad(i, carry):
        cols = pl.ds(pl.multiple_of(i * LANE, LANE), LANE)
        skip = spread_row(skip_ref, i)
        for r in range(RESPS):
            rows = slice(r * RESP_ROWS, (r + 1) * RESP_ROWS)
            b_rows = back[rows, cols]
            within = jnp.dot(
                mix_t[rows, cols], blocks_of(b_rows), preferred_element_type=F32
            )
            gin_ref[rows, cols] = (within + skip * b_rows.astype(F32)).astype(BF16)
        return carry

    lax.fori_loop(0, PAIRS, input_grad, 0)

    def finish_state(s, carry):
        landed(gy_recv.at[s], gy_s.at[s], gy_r.at[s], dev_yh)
        span = pl.ds(pl.multiple_of(chunk_of(z, s) * LANE, LANE), LANE)
        gstate_ref[span, :] = gstate_ref[span, :] + gy_recv[s].astype(F32)
        return carry

    lax.fori_loop(0, NZ, finish_state, 0)

    for n in range(NBLK):
        total = r_own[n, 0]
        for j in (1, 2, 3):
            landed(r_recv.at[j - 1, n], rr_s.at[j - 1, n], rr_r.at[j - 1, n], dev_yl(-j))
            total = total + r_recv[j - 1, n].astype(F32)
        layer_ref[:, n * BLK : (n + 1) * BLK] = total.astype(BF16)

    for copy in pending:
        copy.wait_send()

    def sent(src, dst, ss, rs, dev):
        pltpu.make_async_remote_copy(
            src_ref=src, dst_ref=dst, send_sem=ss, recv_sem=rs, device_id=dev, device_id_type=MESH
        ).wait_send()

    def drain_g(s, carry):
        for j in (1, 2, 3):
            sent(
                g_piece(g_send, j, s), g_piece(g_recv, j, s),
                gx_s.at[j - 1, s], gx_r.at[j - 1, s], dev_x(j),
            )
        sent(gy_send.at[s], gy_recv.at[s], gy_s.at[s], gy_r.at[s], dev_yh)
        return carry

    lax.fori_loop(0, NZ, drain_g, 0)

    def drain_p(n, carry):
        sent(p_send.at[n], p_recv.at[n], pp_s.at[n], pp_r.at[n], dev_core)
        for j in (1, 2, 3):
            sent(
                r_send.at[j - 1, n], r_recv.at[j - 1, n],
                rr_s.at[j - 1, n], rr_r.at[j - 1, n], dev_yl(j),
            )
        return carry

    lax.fori_loop(0, NBLK, drain_p, 0)


def per_device(
    ssm_input,
    b_proj,
    c_proj,
    step_size,
    a_log,
    d_skip,
    out_weight,
    prompt_state,
    prompt_of,
    out_grad,
):
    vmem = pl.BlockSpec(memory_space=pltpu.VMEM)
    anywhere = pl.BlockSpec(memory_space=pl.ANY)
    dma = pltpu.SemaphoreType.DMA
    sems = [
        (),
        (2, 3),
        (2, 4, 2),
        (),
        (2, 2),
        (2, 2),
        (3,),
        (4,),
        (3, NZ),
        (NZ,),
        (NBLK,),
        (3, NBLK),
    ]
    sem_scratch = []
    for shape in sems:
        sem_scratch += [dma(shape), dma(shape)]
    layer_out, grad_input, grad_state = pl.pallas_call(
        kernel,
        out_shape=(
            jax.ShapeDtypeStruct((RESP_ROWS, DW), BF16),
            jax.ShapeDtypeStruct((ROWS, WIDTH), BF16),
            jax.ShapeDtypeStruct((WIDTH, NS), F32),
        ),
        in_specs=[pl.BlockSpec(memory_space=pltpu.SMEM)] + [vmem] * 6 + [anywhere] * 3,
        out_specs=(vmem, vmem, vmem),
        scratch_shapes=[
            pltpu.VMEM((WIDTH, DW), BF16),
            pltpu.VMEM((ROWS, DW), BF16),
            pltpu.VMEM((GROUP, WIDTH, NS), BF16),
            pltpu.VMEM((ROWS, GROUP * NS), BF16),
            pltpu.VMEM((ROWS, WIDTH), BF16),
            pltpu.VMEM((ROWS, WIDTH), BF16),
            pltpu.VMEM((ROWS, WIDTH), F32),
            pltpu.VMEM((ROWS, WIDTH), BF16),
            pltpu.VMEM((ROWS, WIDTH), BF16),
            pltpu.VMEM((ROWS, BLK), F32),
            pltpu.VMEM((NBLK, NYL, RESP_ROWS, BLK), BF16),
            pltpu.VMEM((NBLK, NYL, RESP_ROWS, BLK), BF16),
            pltpu.VMEM((NBLK, NYL, RESP_ROWS, BLK), F32),
            pltpu.VMEM((3, NBLK, RESP_ROWS, BLK), BF16),
            pltpu.VMEM((3, NBLK, RESP_ROWS, BLK), BF16),
            pltpu.VMEM((LANE, GROUP * NS), F32),
            pltpu.VMEM((NZ, NYH, LANE, NS), F32),
            pltpu.VMEM((3, NZ, NYH, LANE, NS), BF16),
            pltpu.VMEM((3, NZ, NYH, LANE, NS), BF16),
            pltpu.VMEM((NZ, LANE, NS), BF16),
            pltpu.VMEM((NZ, LANE, NS), BF16),
            dma((3,)),
        ]
        + sem_scratch,
        compiler_params=pltpu.CompilerParams(
            collective_id=0, has_side_effects=True, vmem_limit_bytes=56 * 1024 * 1024
        ),
        name="ssd_span",
    )(
        prompt_of,
        ssm_input,
        b_proj,
        c_proj,
        step_size,
        a_log.reshape(1, HEADS),
        d_skip.reshape(1, HEADS),
        out_weight,
        prompt_state.reshape(WIDTH, NS),
        out_grad,
    )
    return layer_out, grad_input, grad_state.reshape(1, HEADS, WIDTH // HEADS, NS)


def solution(mesh):
    placed = (
        P("resp", "head"),
        P("resp", "head"),
        P("resp", "head"),
        P("resp", "head"),
        P("head"),
        P("head"),
        P(("head", "resp"), None),
        P("resp", "head", None, None),
        P("resp"),
        P(("resp", "head"), None),
    )
    return jax.shard_map(
        per_device,
        mesh=mesh,
        in_specs=placed,
        out_specs=(P(("resp", "head"), None), P("resp", "head"), P("resp", "head", None, None)),
        check_vma=False,
    )
```

```python
import functools

import jax
import jax.numpy as jnp
from jax import lax
from jax.experimental import pallas as pl
from jax.experimental.pallas import tpu as pltpu
from jax.sharding import PartitionSpec as P

MESH = pl.DeviceIdType.MESH
F32 = jnp.float32
BF16 = jnp.bfloat16
HIGHEST = lax.Precision.HIGHEST

NX, NYH, NZ, NYL, NCORE = 4, 2, 8, 4, 2
GROUP = NX * NYH
RESP_ROWS = 64
RESPS = 8
ROWS = RESP_ROWS * RESPS
NS = 128
HEADS = 16
WIDTH = 1024
DW = 2048
SHARD = 16
LANE = 128
PAIRS = WIDTH // LANE
NBLK = 4
BLK = DW // NBLK
EARLY = BLK
CUT = 1536


def dot_nt(a, b):
    return lax.dot_general(a, b, (((1,), (1,)), ((), ())), preferred_element_type=F32)


def dot_tn(a, b):
    return lax.dot_general(a, b, (((0,), (0,)), ((), ())), preferred_element_type=F32)


def chunk_of(z, s):
    far = (s + 1) // 2
    sign = 1 - 2 * (s % 2)
    return lax.rem(z + NZ + sign * far, NZ)


def kernel(
    prompt_ref,
    step_ref,
    alog_ref,
    skip_ref,
    x_hbm,
    b_hbm,
    c_hbm,
    w_ref,
    state_ref,
    og_ref,
    layer_ref,
    gin_ref,
    gstate_ref,
    x_ref,
    b_ref,
    c_ref,
    steps_ref,
    w_all,
    w_part,
    og_all,
    states,
    csel,
    inner,
    mix,
    mix_t,
    growth,
    ssm,
    back,
    p_tmp,
    p_send,
    p_recv,
    r_own,
    r_send,
    r_recv,
    g_tmp,
    g_own,
    g_send,
    g_recv,
    gy_send,
    gy_recv,
    loc_sem,
    wy_s,
    wy_r,
    wx_s,
    wx_r,
    wz_s,
    wz_r,
    pz_s,
    pz_r,
    vz_s,
    vz_r,
    vx_s,
    vx_r,
    vf_s,
    vf_r,
    sy_s,
    sy_r,
    sx_s,
    sx_r,
    sf_s,
    sf_r,
    oy_s,
    oy_r,
    oc_s,
    oc_r,
    gx_s,
    gx_r,
    gy_s,
    gy_r,
    pp_s,
    pp_r,
    rr_s,
    rr_r,
):
    resp = lax.axis_index("resp")
    head = lax.axis_index("head")
    x = lax.rem(resp, NX)
    yh = lax.rem(resp // NX, NYH)
    z = resp // GROUP
    core = lax.rem(head, NCORE)
    yl = head // NCORE

    def resp_at(z_, yh_, x_):
        return z_ * GROUP + yh_ * NX + x_

    def x_at(j):
        return lax.rem(x + NX + j, NX)

    def z_at(j):
        return lax.rem(z + NZ + j, NZ)

    def dev_x(j):
        return (resp_at(z, yh, x_at(j)), head)

    def dev_z(j):
        return (resp_at(z_at(j), yh, x), head)

    dev_yh = (resp_at(z, 1 - yh, x), head)
    dev_core = (resp, yl * NCORE + 1 - core)

    def dev_yl(j):
        return (resp, (yl + j) * NCORE + core)

    def send(src, dst, ss, rs, dev):
        copy = pltpu.make_async_remote_copy(
            src_ref=src, dst_ref=dst, send_sem=ss, recv_sem=rs, device_id=dev, device_id_type=MESH
        )
        copy.start()
        return copy

    def landed(dst, ss, rs, dev):
        pltpu.make_async_remote_copy(
            src_ref=dst, dst_ref=dst, send_sem=ss, recv_sem=rs, device_id=dev, device_id_type=MESH
        ).wait_recv()

    def sent(src, dst, ss, rs, dev):
        pltpu.make_async_remote_copy(
            src_ref=src, dst_ref=dst, send_sem=ss, recv_sem=rs, device_id=dev, device_id_type=MESH
        ).wait_send()

    pending = []
    SIGNS = ((0, 1), (1, -1))

    def has(j):
        return yl + j < NYL if j > 0 else yl + j >= 0

    barrier = pltpu.get_barrier_semaphore()
    partners = [dev_yh, dev_core] + [dev_z(j) for j in range(1, NZ)]
    partners += [dev_x(j) for j in range(1, NX)]
    partners += [(resp, lax.rem(yl + j, NYL) * NCORE + core) for j in (1, NYL - 1)]
    for dev in partners:
        pl.semaphore_signal(barrier, inc=1, device_id=dev, device_id_type=MESH)
    local = [
        pltpu.make_async_copy(c_hbm, c_ref, loc_sem.at[0]),
        pltpu.make_async_copy(b_hbm, b_ref, loc_sem.at[1]),
    ]
    for copy in local:
        copy.start()
    pl.semaphore_wait(barrier, len(partners))
    def w_rows(z_, yh_, x_):
        return pl.ds(pl.multiple_of(resp_at(z_, yh_, x_) * SHARD, SHARD), SHARD)

    def w_half(z_, yh_):
        start = (z_ * NYH + yh_) * (NX * SHARD)
        return pl.ds(pl.multiple_of(start, NX * SHARD), NX * SHARD)

    def og_rows(h_):
        return og_all.at[pl.ds(pl.multiple_of(h_ * RESP_ROWS, RESP_ROWS), RESP_ROWS), :]

    w_a, w_b = w_ref.at[:, 0:CUT], w_ref.at[:, CUT:DW]
    own_rows, oth_rows = w_rows(z, yh, x), w_rows(z, 1 - yh, x)
    pending.append(send(w_a, w_all.at[own_rows, 0:CUT], wy_s.at[0], wy_r.at[0], dev_yh))
    pending.append(send(w_b, w_part.at[x, z, yh], wy_s.at[1], wy_r.at[1], dev_yh))
    my_slot = yh * NX + x
    pending.append(send(state_ref, states.at[my_slot], sy_s, sy_r, dev_yh))
    for j in (1, 2, 3):
        pending.append(
            send(w_a, w_all.at[own_rows, 0:CUT], wx_s.at[0, j - 1], wx_r.at[0, j - 1], dev_x(j))
        )

    def send_v(half):
        piece = w_part.at[x, z, yh if half == 0 else 1 - yh]
        for j in range(1, NZ):
            pending.append(
                send(
                    w_b if half == 0 else piece, piece,
                    vz_s.at[half, j - 1], vz_r.at[half, j - 1], dev_z(j),
                )
            )

    def land_v(half):
        for j in range(1, NZ):
            piece = w_part.at[x, z_at(-j), yh if half == 0 else 1 - yh]
            landed(piece, vz_s.at[half, j - 1], vz_r.at[half, j - 1], dev_z(-j))

    send_v(0)

    def send_og(i, d, sign):
        @pl.when(jnp.logical_and(has(sign), has(-sign * i)) if i else has(sign))
        def _():
            piece = og_rows((yl - sign * i) * NCORE + core)
            send(og_ref if i == 0 else piece, piece, oy_s.at[d, i], oy_r.at[d, i], dev_yl(sign))

    def drain_og(i, d, sign):
        @pl.when(jnp.logical_and(has(sign), has(-sign * i)) if i else has(sign))
        def _():
            piece = og_rows((yl - sign * i) * NCORE + core)
            sent(og_ref if i == 0 else piece, piece, oy_s.at[d, i], oy_r.at[d, i], dev_yl(sign))

    def land_og(i):
        for d, sign in SIGNS:

            @pl.when(has(-sign * (i + 1)))
            def _():
                piece = og_rows((yl - sign * (i + 1)) * NCORE + core)
                landed(piece, oy_s.at[d, i], oy_r.at[d, i], dev_yl(-sign))
                send(piece, piece, oc_s.at[1 + 3 * d + i], oc_r.at[1 + 3 * d + i], dev_core)

        if i < 2:
            for d, sign in SIGNS:
                send_og(i + 1, d, sign)

    local += [
        pltpu.make_async_copy(w_a, w_all.at[own_rows, 0:CUT], loc_sem.at[2]),
        pltpu.make_async_copy(w_b, w_part.at[x, z, yh], loc_sem.at[3]),
        pltpu.make_async_copy(og_ref, og_rows(head), loc_sem.at[4]),
        pltpu.make_async_copy(state_ref, states.at[my_slot], loc_sem.at[5]),
        pltpu.make_async_copy(x_hbm, x_ref, loc_sem.at[6]),
    ]
    for copy in local[2:]:
        copy.start()

    base = (resp // GROUP) * GROUP
    steps_ref[...] = jnp.transpose(step_ref[...])

    def fill_csel(r, carry):
        rows = pl.ds(pl.multiple_of(r * RESP_ROWS, RESP_ROWS), RESP_ROWS)
        slot = prompt_ref[r] - base
        c_rows = c_ref[rows, :].astype(F32)
        for k in range(GROUP):
            keep = jnp.where(slot == k, 1.0, 0.0).astype(F32)
            csel[rows, k * NS : (k + 1) * NS] = (c_rows * keep).astype(BF16)
        return carry

    row_id = lax.broadcasted_iota(jnp.int32, (RESP_ROWS, LANE), 0)
    lane_id = lax.broadcasted_iota(jnp.int32, (RESP_ROWS, LANE), 1)
    lane_pos = lax.rem(lane_id, RESP_ROWS)
    first = lane_id < RESP_ROWS
    diag = lane_pos == row_id
    earlier = lane_pos <= row_id
    later = lane_pos >= row_id
    tri = (
        lax.broadcasted_iota(jnp.int32, (RESP_ROWS, RESP_ROWS), 0)
        >= lax.broadcasted_iota(jnp.int32, (RESP_ROWS, RESP_ROWS), 1)
    ).astype(F32)
    a_neg = -jnp.exp(alog_ref[...])

    def spread(columns, i):
        return jnp.where(first, columns[:, 2 * i : 2 * i + 1], columns[:, 2 * i + 1 : 2 * i + 2])

    def fill_mix(r, carry):
        rows = pl.ds(pl.multiple_of(r * RESP_ROWS, RESP_ROWS), RESP_ROWS)
        c_rows, b_rows = c_ref[rows, :], b_ref[rows, :]
        steps = steps_ref[rows, :]
        cum = lax.dot_general(
            tri, steps * a_neg, (((1,), (0,)), ((), ())),
            precision=HIGHEST, preferred_element_type=F32,
        )
        score = dot_nt(c_rows, jnp.concatenate([b_rows, b_rows], axis=0))
        score_t = dot_nt(b_rows, jnp.concatenate([c_rows, c_rows], axis=0))
        for i in range(PAIRS):
            cols = slice(i * LANE, (i + 1) * LANE)
            cum_i, step_i = spread(cum, i), spread(steps, i)
            cum_row = jnp.sum(jnp.where(diag, cum_i, 0.0), axis=0, keepdims=True)
            step_row = jnp.sum(jnp.where(diag, step_i, 0.0), axis=0, keepdims=True)
            differ = cum_i - cum_row
            decay = jnp.exp(jnp.where(earlier, differ, 0.0))
            mix[rows, cols] = jnp.where(earlier, decay * step_row * score, 0.0).astype(BF16)
            decay_t = jnp.exp(jnp.where(later, -differ, 0.0))
            mix_t[rows, cols] = jnp.where(later, decay_t * step_i * score_t, 0.0).astype(BF16)
            growth[rows, cols] = jnp.exp(cum_i)
        return carry

    block_mask = (
        (lax.broadcasted_iota(jnp.int32, (LANE, LANE), 0) < RESP_ROWS)
        == (lax.broadcasted_iota(jnp.int32, (LANE, LANE), 1) < RESP_ROWS)
    ).astype(F32).astype(BF16)

    def blocks_of(pair):
        return jnp.concatenate([pair, pair], axis=0) * block_mask

    def z_pieces(step, half, sent_ones):
        yh_ = yh if half == 0 else 1 - yh
        for d, sign in SIGNS:
            if step == 3 and half != d:
                continue
            z_ = z_at(-sign * (step if sent_ones else step + 1))
            piece = w_all.at[w_half(z_, yh_), EARLY:CUT]
            yield piece, wz_s.at[d, step, half], wz_r.at[d, step, half], sign

    def send_z(step, half):
        for piece, ss, rs, sign in z_pieces(step, half, True):
            pending.append(send(piece, piece, ss, rs, dev_z(sign)))

    def land_z(step, half):
        for piece, ss, rs, sign in z_pieces(step, half, False):
            landed(piece, ss, rs, dev_z(-sign))

    def p_pieces(step, sent_ones):
        for d, sign in SIGNS:
            z_ = z_at(-sign * (step if sent_ones else step + 1))
            if step == 3:
                rows = w_half(z_, yh if d == 0 else 1 - yh)
            else:
                rows = pl.ds(pl.multiple_of(z_ * LANE, LANE), LANE)
            yield w_all.at[rows, 0:EARLY], pz_s.at[d, step], pz_r.at[d, step], sign

    def send_p(step):
        for piece, ss, rs, sign in p_pieces(step, True):
            pending.append(send(piece, piece, ss, rs, dev_z(sign)))

    def land_p(step):
        for piece, ss, rs, sign in p_pieces(step, False):
            landed(piece, ss, rs, dev_z(-sign))

    def slot_of(yh_, j):
        return yh_ * NX + x_at(j)

    def send_states(n):
        yh_ = yh if n == 0 else 1 - yh
        piece = states.at[slot_of(yh_, 0)]
        for d, sign in SIGNS:
            pending.append(
                send(
                    state_ref if n == 0 else piece, piece,
                    sx_s.at[n, d], sx_r.at[n, d], dev_x(sign),
                )
            )

    def pass_states(n):
        yh_ = yh if n == 0 else 1 - yh
        for d, sign in SIGNS:
            landed(states.at[slot_of(yh_, -sign)], sx_s.at[n, d], sx_r.at[n, d], dev_x(-sign))
            piece = states.at[slot_of(yh_, -sign), pl.ds(d * (WIDTH // 2), WIDTH // 2), :]
            pending.append(send(piece, piece, sf_s.at[n, d], sf_r.at[n, d], dev_x(sign)))

    def land_states(n):
        yh_ = yh if n == 0 else 1 - yh
        for d, sign in SIGNS:
            piece = states.at[slot_of(yh_, 2), pl.ds(d * (WIDTH // 2), WIDTH // 2), :]
            landed(piece, sf_s.at[n, d], sf_r.at[n, d], dev_x(-sign))

    def part_half(j, d):
        return w_part.at[x_at(j), pl.ds(d * (NZ // 2), NZ // 2)]

    def spread_row(row_ref, i):
        row = row_ref[...]
        where_first = lax.broadcasted_iota(jnp.int32, (1, LANE), 1) < RESP_ROWS
        out = jnp.zeros((1, LANE), F32)
        for h in range(HEADS):
            keep = jnp.where(h // 2 == i, 1.0, 0.0).astype(F32)
            mine = where_first if h % 2 == 0 else jnp.logical_not(where_first)
            out = out + jnp.where(mine, row[:, h : h + 1] * keep, 0.0)
        return out

    def forward_within(i, carry):
        cols = pl.ds(pl.multiple_of(i * LANE, LANE), LANE)
        skip = spread_row(skip_ref, i)
        for r in range(RESPS):
            rows = slice(r * RESP_ROWS, (r + 1) * RESP_ROWS)
            x_rows = x_ref[rows, cols]
            within = jnp.dot(
                mix[rows, cols], blocks_of(x_rows), preferred_element_type=F32
            )
            inner[rows, cols] = within + skip * x_rows.astype(F32)
        return carry

    def carried(i, yh_):
        cols = pl.ds(pl.multiple_of(i * LANE, LANE), LANE)
        init = jnp.concatenate([states[yh_ * NX + k, cols, :] for k in range(NX)], axis=1)
        mine = csel[:, pl.ds(pl.multiple_of(yh_ * (NX * NS), NX * NS), NX * NS)]
        return cols, dot_nt(mine, init) * growth[:, cols]

    def forward_own(i, carry):
        cols, more = carried(i, yh)
        inner[:, cols] = inner[:, cols] + more
        return carry

    def forward_other(i, carry):
        cols, more = carried(i, 1 - yh)
        ssm[:, cols] = (inner[:, cols] + more).astype(BF16)
        return carry

    def g_piece(ref, j, u):
        return ref.at[j - 1, pl.ds(2 * u, 2)]

    def unpack(z_, carry):
        for yh_ in range(NYH):
            for x_ in range(NX):
                w_all[w_rows(z_, yh_, x_), CUT:DW] = w_part[x_, z_, yh_]
        return carry

    def span_of(s_):
        return pl.ds(pl.multiple_of(chunk_of(z, s_) * LANE, LANE), LANE)

    def backward(u, carry):
        spans = [span_of(2 * u + i) for i in range(2)]
        rows = jnp.concatenate([w_all[span, :] for span in spans], axis=0)
        back_f = dot_nt(og_all[...], rows)
        back_b = back_f.astype(BF16)
        for i in range(2):
            back[:, spans[i]] = back_b[:, i * LANE : (i + 1) * LANE]
        grown = jnp.concatenate([growth[:, span] for span in spans], axis=1)
        scaled = (grown * back_b.astype(F32)).astype(BF16)
        g_tmp[...] = dot_tn(scaled, csel[...])
        for j in range(NX):
            for y in range(NYH):
                k = y * NX + lax.rem(x + j, NX)
                for i in range(2):
                    piece = g_tmp[
                        i * LANE : (i + 1) * LANE, pl.ds(pl.multiple_of(k * NS, NS), NS)
                    ]
                    if j == 0:
                        g_own[2 * u + i, y] = piece
                    else:
                        g_send[j - 1, 2 * u + i, y] = piece.astype(BF16)
            if j > 0:
                send(
                    g_piece(g_send, j, u), g_piece(g_recv, j, u),
                    gx_s.at[j - 1, u], gx_r.at[j - 1, u], dev_x(j),
                )
        return carry

    def add_x(u, carry):
        for j in (1, 2, 3):
            landed(g_piece(g_recv, j, u), gx_s.at[j - 1, u], gx_r.at[j - 1, u], dev_x(-j))

        def total(s_, y):
            return g_own[s_, y] + (
                g_recv[0, s_, y].astype(F32)
                + g_recv[1, s_, y].astype(F32)
                + g_recv[2, s_, y].astype(F32)
            )

        for i in range(2):
            gy_send[2 * u + i] = total(2 * u + i, 1 - yh).astype(BF16)
        two = pl.ds(2 * u, 2)
        send(gy_send.at[two], gy_recv.at[two], gy_s.at[u], gy_r.at[u], dev_yh)
        for i in range(2):
            gstate_ref[span_of(2 * u + i), :] = total(2 * u + i, yh)
        return carry

    def give(n):
        for j in range(NYL):
            p_send[n, j] = p_tmp[
                pl.ds(pl.multiple_of((j * NCORE + 1 - core) * RESP_ROWS, RESP_ROWS), RESP_ROWS), :
            ].astype(BF16)
            r_own[n, j] = p_tmp[
                pl.ds(pl.multiple_of((j * NCORE + core) * RESP_ROWS, RESP_ROWS), RESP_ROWS), :
            ]
        send(p_send.at[n], p_recv.at[n], pp_s.at[n], pp_r.at[n], dev_core)

    def project(n, carry):
        cols = pl.ds(pl.multiple_of(n * BLK, BLK), BLK)
        p_tmp[...] = jnp.dot(ssm[...], w_all[:, cols], preferred_element_type=F32)
        give(n)
        return carry

    def share(n, carry):
        landed(p_recv.at[n], pp_s.at[n], pp_r.at[n], dev_core)
        for j in range(NYL):
            r_own[n, j] = r_own[n, j] + p_recv[n, j].astype(F32)
        return carry

    def chain(n, d):
        sign = 1 - 2 * d

        def here(place):
            return jnp.logical_and(place >= 0, place < NYL)

        for o in (3, 2, 1):

            @pl.when(here(yl + sign * o))
            def _():
                total = r_own[n, yl + sign * o]
                r_send[d, o - 1, n] = total.astype(BF16)
                if o < 3:

                    @pl.when(here(yl - sign))
                    def _():
                        landed(
                            r_recv.at[d, o, n], rr_s.at[d, o, n], rr_r.at[d, o, n], dev_yl(-sign)
                        )
                        r_send[d, o - 1, n] = (total + r_recv[d, o, n].astype(F32)).astype(BF16)

                send(
                    r_send.at[d, o - 1, n], r_recv.at[d, o - 1, n],
                    rr_s.at[d, o - 1, n], rr_r.at[d, o - 1, n], dev_yl(sign),
                )

    def finish_layer(n, carry):
        for d, sign in SIGNS:

            @pl.when(has(-sign))
            def _():
                landed(r_recv.at[d, 0, n], rr_s.at[d, 0, n], rr_r.at[d, 0, n], dev_yl(-sign))
                r_own[n, yl] = r_own[n, yl] + r_recv[d, 0, n].astype(F32)

        layer_ref[:, pl.ds(pl.multiple_of(n * BLK, BLK), BLK)] = r_own[n, yl].astype(BF16)
        return carry

    def input_grad(i, carry):
        cols = pl.ds(pl.multiple_of(i * LANE, LANE), LANE)
        skip = spread_row(skip_ref, i)
        for r in range(RESPS):
            rows = slice(r * RESP_ROWS, (r + 1) * RESP_ROWS)
            b_rows = back[rows, cols]
            within = jnp.dot(
                mix_t[rows, cols], blocks_of(b_rows), preferred_element_type=F32
            )
            gin_ref[rows, cols] = (within + skip * b_rows.astype(F32)).astype(BF16)
        return carry

    def finish_state(u, carry):
        two = pl.ds(2 * u, 2)
        landed(gy_recv.at[two], gy_s.at[u], gy_r.at[u], dev_yh)
        for i in range(2):
            span = span_of(2 * u + i)
            gstate_ref[span, :] = gstate_ref[span, :] + gy_recv[2 * u + i].astype(F32)
        return carry

    def run(body, *indices):
        lax.fori_loop(indices[0], indices[-1] + 1, body, 0)

    near = yl // (NYL // 2)

    local[0].wait()
    local[1].wait()
    run(fill_mix, 0, 2)
    landed(w_all.at[oth_rows, 0:CUT], wy_s.at[0], wy_r.at[0], dev_yh)
    for j in (1, 2, 3):
        piece = w_all.at[oth_rows, 0:CUT]
        pending.append(send(piece, piece, wx_s.at[1, j - 1], wx_r.at[1, j - 1], dev_x(j)))
    landed(w_part.at[x, z, 1 - yh], wy_s.at[1], wy_r.at[1], dev_yh)
    send_v(1)
    send_states(0)
    run(fill_mix, 3, 4)
    local[2].wait()
    for n, yh_ in enumerate((yh, 1 - yh)):
        for j in (1, 2, 3):
            piece = w_all.at[w_rows(z, yh_, x_at(-j)), 0:CUT]
            landed(piece, wx_s.at[n, j - 1], wx_r.at[n, j - 1], dev_x(-j))
    send_p(0)
    send_z(0, 0)
    for d, sign in SIGNS:
        send_og(0, d, sign)
    pending.append(send(og_ref, og_rows(head), oc_s.at[0], oc_r.at[0], dev_core))

    run(fill_csel, 0, RESPS - 1)
    run(fill_mix, 5, 6)
    land_p(0)
    send_p(1)
    send_z(0, 1)
    run(fill_mix, 7)
    landed(states.at[slot_of(1 - yh, 0)], sy_s, sy_r, dev_yh)
    send_states(1)
    land_p(1)
    send_p(2)
    land_z(0, 0)
    send_z(1, 0)
    land_og(0)
    local[3].wait()
    land_v(0)
    land_v(1)
    for d, sign in SIGNS:
        piece = w_part.at[x]
        pending.append(send(piece, piece, vx_s.at[d], vx_r.at[d], dev_x(sign)))
    local[6].wait()
    run(forward_within, 0, 3)
    land_z(0, 1)
    send_z(1, 1)
    pass_states(0)
    land_og(1)
    land_p(2)
    send_p(3)
    land_z(1, 0)
    send_z(2, 0)
    run(forward_within, 4, 7)
    pass_states(1)
    land_z(1, 1)
    send_z(2, 1)
    for d, sign in SIGNS:
        landed(w_part.at[x_at(-sign)], vx_s.at[d], vx_r.at[d], dev_x(-sign))
        piece = part_half(-sign, d)
        pending.append(send(piece, piece, vf_s.at[d], vf_r.at[d], dev_x(sign)))
    local[5].wait()
    land_states(0)
    run(forward_own, 0, PAIRS - 1)
    land_og(2)
    land_p(3)
    land_z(2, 0)
    send_z(3, 0)
    land_states(1)
    run(forward_other, 0, PAIRS - 1)
    land_z(2, 1)
    send_z(3, 1)
    for d, sign in SIGNS:
        landed(part_half(2, d), vf_s.at[d], vf_r.at[d], dev_x(-sign))
    run(unpack, 0, NZ - 1)
    run(project, 3)
    run(project, 0)
    local[4].wait()
    landed(og_rows(yl * NCORE + 1 - core), oc_s.at[0], oc_r.at[0], dev_core)
    for d, sign in SIGNS:
        for i in range(3):

            @pl.when(has(-sign * (i + 1)))
            def _():
                piece = og_rows((yl - sign * (i + 1)) * NCORE + 1 - core)
                landed(piece, oc_s.at[1 + 3 * d + i], oc_r.at[1 + 3 * d + i], dev_core)

    run(backward, 0)
    share(3, 0)
    chain(3, near)
    share(0, 0)
    run(backward, 1)
    chain(0, near)
    chain(3, 1 - near)
    land_z(3, 0)
    land_z(3, 1)
    run(project, 1, 2)
    run(backward, 2)
    share(1, 0)
    chain(1, near)
    chain(0, 1 - near)
    run(add_x, 0)
    run(backward, 3)
    share(2, 0)
    chain(2, near)
    chain(1, 1 - near)
    run(add_x, 1)
    chain(2, 1 - near)
    run(add_x, 2)
    run(input_grad, 0, PAIRS - 1)
    run(add_x, 3)
    run(finish_layer, 0, NBLK - 1)
    run(finish_state, 0, NZ // 2 - 1)

    for copy in pending:
        copy.wait_send()
    for d, sign in SIGNS:
        for i in range(3):
            drain_og(i, d, sign)

            @pl.when(has(-sign * (i + 1)))
            def _():
                piece = og_rows((yl - sign * (i + 1)) * NCORE + core)
                sent(piece, piece, oc_s.at[1 + 3 * d + i], oc_r.at[1 + 3 * d + i], dev_core)

    def drain_g(u, carry):
        for j in (1, 2, 3):
            sent(
                g_piece(g_send, j, u), g_piece(g_recv, j, u),
                gx_s.at[j - 1, u], gx_r.at[j - 1, u], dev_x(j),
            )
        two = pl.ds(2 * u, 2)
        sent(gy_send.at[two], gy_recv.at[two], gy_s.at[u], gy_r.at[u], dev_yh)
        return carry

    run(drain_g, 0, NZ // 2 - 1)

    def drain_p(n, carry):
        sent(p_send.at[n], p_recv.at[n], pp_s.at[n], pp_r.at[n], dev_core)
        for d, sign in SIGNS:
            for o in (1, 2, 3):

                @pl.when(has(sign * o))
                def _():
                    sent(
                        r_send.at[d, o - 1, n], r_recv.at[d, o - 1, n],
                        rr_s.at[d, o - 1, n], rr_r.at[d, o - 1, n], dev_yl(sign),
                    )

        return carry

    run(drain_p, 0, NBLK - 1)


def copy_out(a, b, c, a_out, b_out, c_out):
    a_out[...] = a[...]
    b_out[...] = b[...]
    c_out[...] = c[...]


def per_device(
    ssm_input,
    b_proj,
    c_proj,
    step_size,
    a_log,
    d_skip,
    out_weight,
    prompt_state,
    prompt_of,
    out_grad,
):
    vmem = pl.BlockSpec(memory_space=pltpu.VMEM)
    anywhere = pl.BlockSpec(memory_space=pl.ANY)
    dma = pltpu.SemaphoreType.DMA
    sems = [
        (2,),
        (2, 3),
        (2, 4, 2),
        (2, 4),
        (2, NZ - 1),
        (2,),
        (2,),
        (),
        (2, 2),
        (2, 2),
        (2, 3),
        (7,),
        (3, NZ // 2),
        (NZ // 2,),
        (NBLK,),
        (2, 3, NBLK),
    ]
    sem_scratch = []
    for shape in sems:
        sem_scratch += [dma(shape), dma(shape)]
    shapes = (
        jax.ShapeDtypeStruct((RESP_ROWS, DW), BF16),
        jax.ShapeDtypeStruct((ROWS, WIDTH), BF16),
        jax.ShapeDtypeStruct((WIDTH, NS), F32),
    )
    results = pl.pallas_call(
        kernel,
        out_shape=shapes,
        in_specs=[pl.BlockSpec(memory_space=pltpu.SMEM)] + [vmem] * 3 + [anywhere] * 6,
        out_specs=(vmem, vmem, vmem),
        scratch_shapes=[
            pltpu.VMEM((ROWS, WIDTH), BF16),
            pltpu.VMEM((ROWS, NS), BF16),
            pltpu.VMEM((ROWS, NS), BF16),
            pltpu.VMEM((ROWS, HEADS), F32),
            pltpu.VMEM((WIDTH, DW), BF16),
            pltpu.VMEM((NX, NZ, NYH, SHARD, DW - CUT), BF16),
            pltpu.VMEM((ROWS, DW), BF16),
            pltpu.VMEM((GROUP, WIDTH, NS), BF16),
            pltpu.VMEM((ROWS, GROUP * NS), BF16),
            pltpu.VMEM((ROWS, WIDTH), F32),
            pltpu.VMEM((ROWS, WIDTH), BF16),
            pltpu.VMEM((ROWS, WIDTH), BF16),
            pltpu.VMEM((ROWS, WIDTH), F32),
            pltpu.VMEM((ROWS, WIDTH), BF16),
            pltpu.VMEM((ROWS, WIDTH), BF16),
            pltpu.VMEM((ROWS, BLK), F32),
            pltpu.VMEM((NBLK, NYL, RESP_ROWS, BLK), BF16),
            pltpu.VMEM((NBLK, NYL, RESP_ROWS, BLK), BF16),
            pltpu.VMEM((NBLK, NYL, RESP_ROWS, BLK), F32),
            pltpu.VMEM((2, 3, NBLK, RESP_ROWS, BLK), BF16),
            pltpu.VMEM((2, 3, NBLK, RESP_ROWS, BLK), BF16),
            pltpu.VMEM((2 * LANE, GROUP * NS), F32),
            pltpu.VMEM((NZ, NYH, LANE, NS), F32),
            pltpu.VMEM((3, NZ, NYH, LANE, NS), BF16),
            pltpu.VMEM((3, NZ, NYH, LANE, NS), BF16),
            pltpu.VMEM((NZ, LANE, NS), BF16),
            pltpu.VMEM((NZ, LANE, NS), BF16),
            dma((7,)),
        ]
        + sem_scratch,
        compiler_params=pltpu.CompilerParams(
            collective_id=0, has_side_effects=True, vmem_limit_bytes=56 * 1024 * 1024
        ),
        name="ssd_span",
    )(
        prompt_of,
        step_size.T,
        a_log.reshape(1, HEADS),
        d_skip.reshape(1, HEADS),
        ssm_input,
        b_proj,
        c_proj,
        out_weight,
        prompt_state.reshape(WIDTH, NS),
        out_grad,
    )
    parts = 4
    blocks = [
        pl.BlockSpec((shape.shape[0] // parts, shape.shape[1]), lambda i: (i, 0))
        for shape in shapes
    ]
    layer_out, grad_input, grad_state = pl.pallas_call(
        copy_out,
        grid=(parts,),
        out_shape=shapes,
        in_specs=blocks,
        out_specs=blocks,
        name="hand_out",
    )(*results)
    return layer_out, grad_input, grad_state.reshape(1, HEADS, WIDTH // HEADS, NS)


def solution(mesh):
    placed = (
        P("resp", "head"),
        P("resp", "head"),
        P("resp", "head"),
        P("resp", "head"),
        P("head"),
        P("head"),
        P(("head", "resp"), None),
        P("resp", "head", None, None),
        P("resp"),
        P(("resp", "head"), None),
    )
    return jax.shard_map(
        per_device,
        mesh=mesh,
        in_specs=placed,
        out_specs=(P(("resp", "head"), None), P("resp", "head"), P("resp", "head", None, None)),
        check_vma=False,
    )
```

```python
import functools

import jax
import jax.numpy as jnp
from jax import lax
from jax.experimental import pallas as pl
from jax.experimental.pallas import tpu as pltpu
from jax.sharding import PartitionSpec as P

MESH = pl.DeviceIdType.MESH
F32 = jnp.float32
BF16 = jnp.bfloat16
HIGHEST = lax.Precision.HIGHEST

NX, NYH, NZ, NYL, NCORE = 4, 2, 8, 4, 2
GROUP = NX * NYH
RESP_ROWS = 64
RESPS = 8
ROWS = RESP_ROWS * RESPS
NS = 128
HEADS = 16
WIDTH = 1024
DW = 2048
SHARD = 16
LANE = 128
PAIRS = WIDTH // LANE
PARTS = 2
NBLK = 4
BLK = DW // NBLK
EARLY = BLK
CUT = 1536


def dot_nt(a, b):
    return lax.dot_general(a, b, (((1,), (1,)), ((), ())), preferred_element_type=F32)


def dot_tn(a, b):
    return lax.dot_general(a, b, (((0,), (0,)), ((), ())), preferred_element_type=F32)


def chunk_of(z, s):
    far = (s + 1) // 2
    sign = 1 - 2 * (s % 2)
    return lax.rem(z + NZ + sign * far, NZ)


def kernel(
    prompt_ref,
    step_ref,
    alog_ref,
    skip_ref,
    x_hbm,
    b_hbm,
    c_hbm,
    w_ref,
    state_ref,
    og_ref,
    layer_ref,
    gin_ref,
    gstate_ref,
    x_ref,
    b_ref,
    c_ref,
    steps_ref,
    w_all,
    w_part,
    og_all,
    states,
    csel,
    inner,
    mix,
    mix_t,
    growth,
    ssm,
    back,
    p_tmp,
    p_send,
    p_recv,
    r_own,
    r_send,
    r_recv,
    g_tmp,
    g_own,
    g_send,
    g_recv,
    gy_send,
    gy_recv,
    loc_sem,
    wy_s,
    wy_r,
    wx_s,
    wx_r,
    wz_s,
    wz_r,
    pz_s,
    pz_r,
    vz_s,
    vz_r,
    vx_s,
    vx_r,
    vf_s,
    vf_r,
    sy_s,
    sy_r,
    sx_s,
    sx_r,
    sf_s,
    sf_r,
    oy_s,
    oy_r,
    oc_s,
    oc_r,
    gx_s,
    gx_r,
    gy_s,
    gy_r,
    pp_s,
    pp_r,
    rr_s,
    rr_r,
):
    resp = lax.axis_index("resp")
    head = lax.axis_index("head")
    x = lax.rem(resp, NX)
    yh = lax.rem(resp // NX, NYH)
    z = resp // GROUP
    core = lax.rem(head, NCORE)
    yl = head // NCORE

    def resp_at(z_, yh_, x_):
        return z_ * GROUP + yh_ * NX + x_

    def x_at(j):
        return lax.rem(x + NX + j, NX)

    def z_at(j):
        return lax.rem(z + NZ + j, NZ)

    def dev_x(j):
        return (resp_at(z, yh, x_at(j)), head)

    def dev_z(j):
        return (resp_at(z_at(j), yh, x), head)

    dev_yh = (resp_at(z, 1 - yh, x), head)
    dev_core = (resp, yl * NCORE + 1 - core)

    def dev_yl(j):
        return (resp, (yl + j) * NCORE + core)

    def send(src, dst, ss, rs, dev):
        copy = pltpu.make_async_remote_copy(
            src_ref=src, dst_ref=dst, send_sem=ss, recv_sem=rs, device_id=dev, device_id_type=MESH
        )
        copy.start()
        return copy

    def landed(dst, ss, rs, dev):
        pltpu.make_async_remote_copy(
            src_ref=dst, dst_ref=dst, send_sem=ss, recv_sem=rs, device_id=dev, device_id_type=MESH
        ).wait_recv()

    def sent(src, dst, ss, rs, dev):
        pltpu.make_async_remote_copy(
            src_ref=src, dst_ref=dst, send_sem=ss, recv_sem=rs, device_id=dev, device_id_type=MESH
        ).wait_send()

    pending = []
    SIGNS = ((0, 1), (1, -1))

    def has(j):
        return yl + j < NYL if j > 0 else yl + j >= 0

    barrier = pltpu.get_barrier_semaphore()
    partners = [dev_yh, dev_core] + [dev_z(j) for j in range(1, NZ)]
    partners += [dev_x(j) for j in range(1, NX)]
    partners += [(resp, lax.rem(yl + j, NYL) * NCORE + core) for j in (1, NYL - 1)]
    for dev in partners:
        pl.semaphore_signal(barrier, inc=1, device_id=dev, device_id_type=MESH)
    local = [
        pltpu.make_async_copy(c_hbm, c_ref, loc_sem.at[0]),
        pltpu.make_async_copy(b_hbm, b_ref, loc_sem.at[1]),
    ]
    for copy in local:
        copy.start()
    pl.semaphore_wait(barrier, len(partners))
    def w_rows(z_, yh_, x_):
        return pl.ds(pl.multiple_of(resp_at(z_, yh_, x_) * SHARD, SHARD), SHARD)

    def w_half(z_, yh_):
        start = (z_ * NYH + yh_) * (NX * SHARD)
        return pl.ds(pl.multiple_of(start, NX * SHARD), NX * SHARD)

    def og_rows(h_):
        return og_all.at[pl.ds(pl.multiple_of(h_ * RESP_ROWS, RESP_ROWS), RESP_ROWS), :]

    w_a, w_b = w_ref.at[:, 0:CUT], w_ref.at[:, CUT:DW]
    own_rows, oth_rows = w_rows(z, yh, x), w_rows(z, 1 - yh, x)
    pending.append(send(w_a, w_all.at[own_rows, 0:CUT], wy_s.at[0], wy_r.at[0], dev_yh))
    pending.append(send(w_b, w_part.at[x, z, yh], wy_s.at[1], wy_r.at[1], dev_yh))
    my_slot = yh * NX + x
    pending.append(send(state_ref, states.at[my_slot], sy_s, sy_r, dev_yh))
    for j in (1, 2, 3):
        pending.append(
            send(w_a, w_all.at[own_rows, 0:CUT], wx_s.at[0, j - 1], wx_r.at[0, j - 1], dev_x(j))
        )

    def send_v(half):
        piece = w_part.at[x, z, yh if half == 0 else 1 - yh]
        for j in range(1, NZ):
            pending.append(
                send(
                    w_b if half == 0 else piece, piece,
                    vz_s.at[half, j - 1], vz_r.at[half, j - 1], dev_z(j),
                )
            )

    def land_v(half):
        for j in range(1, NZ):
            piece = w_part.at[x, z_at(-j), yh if half == 0 else 1 - yh]
            landed(piece, vz_s.at[half, j - 1], vz_r.at[half, j - 1], dev_z(-j))

    send_v(0)

    def send_og(i, d, sign):
        @pl.when(jnp.logical_and(has(sign), has(-sign * i)) if i else has(sign))
        def _():
            piece = og_rows((yl - sign * i) * NCORE + core)
            send(og_ref if i == 0 else piece, piece, oy_s.at[d, i], oy_r.at[d, i], dev_yl(sign))

    def drain_og(i, d, sign):
        @pl.when(jnp.logical_and(has(sign), has(-sign * i)) if i else has(sign))
        def _():
            piece = og_rows((yl - sign * i) * NCORE + core)
            sent(og_ref if i == 0 else piece, piece, oy_s.at[d, i], oy_r.at[d, i], dev_yl(sign))

    def land_og(i):
        for d, sign in SIGNS:

            @pl.when(has(-sign * (i + 1)))
            def _():
                piece = og_rows((yl - sign * (i + 1)) * NCORE + core)
                landed(piece, oy_s.at[d, i], oy_r.at[d, i], dev_yl(-sign))
                send(piece, piece, oc_s.at[1 + 3 * d + i], oc_r.at[1 + 3 * d + i], dev_core)

        if i < 2:
            for d, sign in SIGNS:
                send_og(i + 1, d, sign)

    local += [
        pltpu.make_async_copy(w_a, w_all.at[own_rows, 0:CUT], loc_sem.at[2]),
        pltpu.make_async_copy(w_b, w_part.at[x, z, yh], loc_sem.at[3]),
        pltpu.make_async_copy(og_ref, og_rows(head), loc_sem.at[4]),
        pltpu.make_async_copy(state_ref, states.at[my_slot], loc_sem.at[5]),
        pltpu.make_async_copy(x_hbm, x_ref, loc_sem.at[6]),
    ]
    for copy in local[2:]:
        copy.start()

    base = (resp // GROUP) * GROUP
    steps_ref[...] = jnp.transpose(step_ref[...])

    def fill_csel(r, carry):
        rows = pl.ds(pl.multiple_of(r * RESP_ROWS, RESP_ROWS), RESP_ROWS)
        slot = prompt_ref[r] - base
        c_rows = c_ref[rows, :].astype(F32)
        for k in range(GROUP):
            keep = jnp.where(slot == k, 1.0, 0.0).astype(F32)
            csel[rows, k * NS : (k + 1) * NS] = (c_rows * keep).astype(BF16)
        return carry

    row_id = lax.broadcasted_iota(jnp.int32, (RESP_ROWS, LANE), 0)
    lane_id = lax.broadcasted_iota(jnp.int32, (RESP_ROWS, LANE), 1)
    lane_pos = lax.rem(lane_id, RESP_ROWS)
    first = lane_id < RESP_ROWS
    diag = lane_pos == row_id
    earlier = lane_pos <= row_id
    later = lane_pos >= row_id
    tri = (
        lax.broadcasted_iota(jnp.int32, (RESP_ROWS, RESP_ROWS), 0)
        >= lax.broadcasted_iota(jnp.int32, (RESP_ROWS, RESP_ROWS), 1)
    ).astype(F32)
    a_neg = -jnp.exp(alog_ref[...])

    def spread(columns, i):
        return jnp.where(first, columns[:, 2 * i : 2 * i + 1], columns[:, 2 * i + 1 : 2 * i + 2])

    def fill_mix(r, carry):
        rows = pl.ds(pl.multiple_of(r * RESP_ROWS, RESP_ROWS), RESP_ROWS)
        c_rows, b_rows = c_ref[rows, :], b_ref[rows, :]
        steps = steps_ref[rows, :]
        cum = lax.dot_general(
            tri, steps * a_neg, (((1,), (0,)), ((), ())),
            precision=HIGHEST, preferred_element_type=F32,
        )
        score = dot_nt(c_rows, jnp.concatenate([b_rows, b_rows], axis=0))
        score_t = dot_nt(b_rows, jnp.concatenate([c_rows, c_rows], axis=0))
        for i in range(PAIRS):
            cols = slice(i * LANE, (i + 1) * LANE)
            cum_i, step_i = spread(cum, i), spread(steps, i)
            cum_row = jnp.sum(jnp.where(diag, cum_i, 0.0), axis=0, keepdims=True)
            step_row = jnp.sum(jnp.where(diag, step_i, 0.0), axis=0, keepdims=True)
            differ = cum_i - cum_row
            decay = jnp.exp(jnp.where(earlier, differ, 0.0))
            mix[rows, cols] = jnp.where(earlier, decay * step_row * score, 0.0).astype(BF16)
            decay_t = jnp.exp(jnp.where(later, -differ, 0.0))
            mix_t[rows, cols] = jnp.where(later, decay_t * step_i * score_t, 0.0).astype(BF16)
            growth[rows, cols] = jnp.exp(cum_i)
        return carry

    block_mask = (
        (lax.broadcasted_iota(jnp.int32, (LANE, LANE), 0) < RESP_ROWS)
        == (lax.broadcasted_iota(jnp.int32, (LANE, LANE), 1) < RESP_ROWS)
    ).astype(F32).astype(BF16)

    def blocks_of(pair):
        return jnp.concatenate([pair, pair], axis=0) * block_mask

    def z_pieces(step, half, sent_ones):
        yh_ = yh if half == 0 else 1 - yh
        for d, sign in SIGNS:
            if step == 3 and half != d:
                continue
            z_ = z_at(-sign * (step if sent_ones else step + 1))
            piece = w_all.at[w_half(z_, yh_), EARLY:CUT]
            yield piece, wz_s.at[d, step, half], wz_r.at[d, step, half], sign

    def send_z(step, half):
        for piece, ss, rs, sign in z_pieces(step, half, True):
            pending.append(send(piece, piece, ss, rs, dev_z(sign)))

    def land_z(step, half):
        for piece, ss, rs, sign in z_pieces(step, half, False):
            landed(piece, ss, rs, dev_z(-sign))

    def p_pieces(step, sent_ones):
        for d, sign in SIGNS:
            z_ = z_at(-sign * (step if sent_ones else step + 1))
            if step == 3:
                rows = w_half(z_, yh if d == 0 else 1 - yh)
            else:
                rows = pl.ds(pl.multiple_of(z_ * LANE, LANE), LANE)
            yield w_all.at[rows, 0:EARLY], pz_s.at[d, step], pz_r.at[d, step], sign

    def send_p(step):
        for piece, ss, rs, sign in p_pieces(step, True):
            pending.append(send(piece, piece, ss, rs, dev_z(sign)))

    def land_p(step):
        for piece, ss, rs, sign in p_pieces(step, False):
            landed(piece, ss, rs, dev_z(-sign))

    def slot_of(yh_, j):
        return yh_ * NX + x_at(j)

    def send_states(n):
        yh_ = yh if n == 0 else 1 - yh
        piece = states.at[slot_of(yh_, 0)]
        for d, sign in SIGNS:
            pending.append(
                send(
                    state_ref if n == 0 else piece, piece,
                    sx_s.at[n, d], sx_r.at[n, d], dev_x(sign),
                )
            )

    def pass_states(n):
        yh_ = yh if n == 0 else 1 - yh
        for d, sign in SIGNS:
            landed(states.at[slot_of(yh_, -sign)], sx_s.at[n, d], sx_r.at[n, d], dev_x(-sign))
            piece = states.at[slot_of(yh_, -sign), pl.ds(d * (WIDTH // 2), WIDTH // 2), :]
            pending.append(send(piece, piece, sf_s.at[n, d], sf_r.at[n, d], dev_x(sign)))

    def land_states(n):
        yh_ = yh if n == 0 else 1 - yh
        for d, sign in SIGNS:
            piece = states.at[slot_of(yh_, 2), pl.ds(d * (WIDTH // 2), WIDTH // 2), :]
            landed(piece, sf_s.at[n, d], sf_r.at[n, d], dev_x(-sign))

    def part_half(j, d):
        return w_part.at[x_at(j), pl.ds(d * (NZ // 2), NZ // 2)]

    def spread_row(row_ref, i):
        row = row_ref[...]
        where_first = lax.broadcasted_iota(jnp.int32, (1, LANE), 1) < RESP_ROWS
        out = jnp.zeros((1, LANE), F32)
        for h in range(HEADS):
            keep = jnp.where(h // 2 == i, 1.0, 0.0).astype(F32)
            mine = where_first if h % 2 == 0 else jnp.logical_not(where_first)
            out = out + jnp.where(mine, row[:, h : h + 1] * keep, 0.0)
        return out

    def forward_within(i, carry):
        cols = pl.ds(pl.multiple_of(i * LANE, LANE), LANE)
        skip = spread_row(skip_ref, i)
        for r in range(RESPS):
            rows = slice(r * RESP_ROWS, (r + 1) * RESP_ROWS)
            x_rows = x_ref[rows, cols]
            within = jnp.dot(
                mix[rows, cols], blocks_of(x_rows), preferred_element_type=F32
            )
            inner[rows, cols] = within + skip * x_rows.astype(F32)
        return carry

    def carried(i, yh_):
        cols = pl.ds(pl.multiple_of(i * (2 * LANE), 2 * LANE), 2 * LANE)
        init = jnp.concatenate([states[yh_ * NX + k, cols, :] for k in range(NX)], axis=1)
        mine = csel[:, pl.ds(pl.multiple_of(yh_ * (NX * NS), NX * NS), NX * NS)]
        return cols, dot_nt(mine, init) * growth[:, cols]

    def forward_own(i, carry):
        cols, more = carried(i, yh)
        inner[:, cols] = inner[:, cols] + more
        return carry

    def forward_other(i, carry):
        cols, more = carried(i, 1 - yh)
        ssm[:, cols] = (inner[:, cols] + more).astype(BF16)
        return carry

    def g_piece(ref, j, u):
        return ref.at[j - 1, pl.ds(2 * u, 2)]

    def unpack(z_, carry):
        for yh_ in range(NYH):
            for x_ in range(NX):
                w_all[w_rows(z_, yh_, x_), CUT:DW] = w_part[x_, z_, yh_]
        return carry

    def span_of(s_):
        return pl.ds(pl.multiple_of(chunk_of(z, s_) * LANE, LANE), LANE)

    def backward(u, carry):
        spans = [span_of(2 * u + i) for i in range(2)]
        rows = jnp.concatenate([w_all[span, :] for span in spans], axis=0)
        back_f = dot_nt(og_all[...], rows)
        back_b = back_f.astype(BF16)
        for i in range(2):
            back[:, spans[i]] = back_b[:, i * LANE : (i + 1) * LANE]
        grown = jnp.concatenate([growth[:, span] for span in spans], axis=1)
        scaled = (grown * back_b.astype(F32)).astype(BF16)
        g_tmp[...] = dot_tn(scaled, csel[...])
        for j in range(NX):
            for y in range(NYH):
                k = y * NX + lax.rem(x + j, NX)
                for i in range(2):
                    piece = g_tmp[
                        i * LANE : (i + 1) * LANE, pl.ds(pl.multiple_of(k * NS, NS), NS)
                    ]
                    if j == 0:
                        g_own[2 * u + i, y] = piece
                    else:
                        g_send[j - 1, 2 * u + i, y] = piece.astype(BF16)
            if j > 0:
                send(
                    g_piece(g_send, j, u), g_piece(g_recv, j, u),
                    gx_s.at[j - 1, u], gx_r.at[j - 1, u], dev_x(j),
                )
        return carry

    def add_x(u, carry):
        for j in (1, 2, 3):
            landed(g_piece(g_recv, j, u), gx_s.at[j - 1, u], gx_r.at[j - 1, u], dev_x(-j))

        def total(s_, y):
            return g_own[s_, y] + (
                g_recv[0, s_, y].astype(F32)
                + g_recv[1, s_, y].astype(F32)
                + g_recv[2, s_, y].astype(F32)
            )

        for i in range(2):
            gy_send[2 * u + i] = total(2 * u + i, 1 - yh).astype(BF16)
        two = pl.ds(2 * u, 2)
        send(gy_send.at[two], gy_recv.at[two], gy_s.at[u], gy_r.at[u], dev_yh)
        for i in range(2):
            gstate_ref[span_of(2 * u + i), :] = total(2 * u + i, yh)
        return carry

    def give(n):
        for j in range(NYL):
            p_send[n, j] = p_tmp[
                pl.ds(pl.multiple_of((j * NCORE + 1 - core) * RESP_ROWS, RESP_ROWS), RESP_ROWS), :
            ].astype(BF16)
            r_own[n, j] = p_tmp[
                pl.ds(pl.multiple_of((j * NCORE + core) * RESP_ROWS, RESP_ROWS), RESP_ROWS), :
            ]
        send(p_send.at[n], p_recv.at[n], pp_s.at[n], pp_r.at[n], dev_core)

    def project(n, carry):
        cols = pl.ds(pl.multiple_of(n * BLK, BLK), BLK)
        p_tmp[...] = jnp.dot(ssm[...], w_all[:, cols], preferred_element_type=F32)
        give(n)
        return carry

    def share(n, carry):
        landed(p_recv.at[n], pp_s.at[n], pp_r.at[n], dev_core)
        for j in range(NYL):
            r_own[n, j] = r_own[n, j] + p_recv[n, j].astype(F32)
        return carry

    def chain(n, d):
        sign = 1 - 2 * d

        def here(place):
            return jnp.logical_and(place >= 0, place < NYL)

        for o in (3, 2, 1):

            @pl.when(here(yl + sign * o))
            def _():
                total = r_own[n, yl + sign * o]
                r_send[d, o - 1, n] = total.astype(BF16)
                if o < 3:

                    @pl.when(here(yl - sign))
                    def _():
                        landed(
                            r_recv.at[d, o, n], rr_s.at[d, o, n], rr_r.at[d, o, n], dev_yl(-sign)
                        )
                        r_send[d, o - 1, n] = (total + r_recv[d, o, n].astype(F32)).astype(BF16)

                send(
                    r_send.at[d, o - 1, n], r_recv.at[d, o - 1, n],
                    rr_s.at[d, o - 1, n], rr_r.at[d, o - 1, n], dev_yl(sign),
                )

    def finish_layer(n, carry):
        for d, sign in SIGNS:

            @pl.when(has(-sign))
            def _():
                landed(r_recv.at[d, 0, n], rr_s.at[d, 0, n], rr_r.at[d, 0, n], dev_yl(-sign))
                r_own[n, yl] = r_own[n, yl] + r_recv[d, 0, n].astype(F32)

        layer_ref[:, pl.ds(pl.multiple_of(n * BLK, BLK), BLK)] = r_own[n, yl].astype(BF16)
        return carry

    def input_grad(i, carry):
        cols = pl.ds(pl.multiple_of(i * LANE, LANE), LANE)
        skip = spread_row(skip_ref, i)
        for r in range(RESPS):
            rows = slice(r * RESP_ROWS, (r + 1) * RESP_ROWS)
            b_rows = back[rows, cols]
            within = jnp.dot(
                mix_t[rows, cols], blocks_of(b_rows), preferred_element_type=F32
            )
            gin_ref[rows, cols] = (within + skip * b_rows.astype(F32)).astype(BF16)
        return carry

    def finish_state(u, carry):
        two = pl.ds(2 * u, 2)
        landed(gy_recv.at[two], gy_s.at[u], gy_r.at[u], dev_yh)
        for i in range(2):
            span = span_of(2 * u + i)
            gstate_ref[span, :] = gstate_ref[span, :] + gy_recv[2 * u + i].astype(F32)
        return carry

    def run(body, *indices):
        lax.fori_loop(indices[0], indices[-1] + 1, body, 0)

    near = yl // (NYL // 2)

    local[0].wait()
    local[1].wait()
    run(fill_mix, 0, 2)
    landed(w_all.at[oth_rows, 0:CUT], wy_s.at[0], wy_r.at[0], dev_yh)
    for j in (1, 2, 3):
        piece = w_all.at[oth_rows, 0:CUT]
        pending.append(send(piece, piece, wx_s.at[1, j - 1], wx_r.at[1, j - 1], dev_x(j)))
    landed(w_part.at[x, z, 1 - yh], wy_s.at[1], wy_r.at[1], dev_yh)
    send_v(1)
    send_states(0)
    for d, sign in SIGNS:
        send_og(0, d, sign)
    pending.append(send(og_ref, og_rows(head), oc_s.at[0], oc_r.at[0], dev_core))
    run(fill_mix, 3, 4)
    local[2].wait()
    for n, yh_ in enumerate((yh, 1 - yh)):
        for j in (1, 2, 3):
            piece = w_all.at[w_rows(z, yh_, x_at(-j)), 0:CUT]
            landed(piece, wx_s.at[n, j - 1], wx_r.at[n, j - 1], dev_x(-j))
    send_p(0)
    send_z(0, 0)

    run(fill_csel, 0, RESPS - 1)
    run(fill_mix, 5, 6)
    land_p(0)
    send_p(1)
    send_z(0, 1)
    run(fill_mix, 7)
    land_og(0)
    landed(states.at[slot_of(1 - yh, 0)], sy_s, sy_r, dev_yh)
    send_states(1)
    land_p(1)
    send_p(2)
    land_z(0, 0)
    send_z(1, 0)
    local[3].wait()
    land_v(0)
    land_v(1)
    for d, sign in SIGNS:
        piece = w_part.at[x]
        pending.append(send(piece, piece, vx_s.at[d], vx_r.at[d], dev_x(sign)))
    local[6].wait()
    run(forward_within, 0, 3)
    land_z(0, 1)
    send_z(1, 1)
    pass_states(0)
    land_og(1)
    land_p(2)
    send_p(3)
    land_z(1, 0)
    send_z(2, 0)
    run(forward_within, 4, 7)
    pass_states(1)
    land_z(1, 1)
    send_z(2, 1)
    for d, sign in SIGNS:
        landed(w_part.at[x_at(-sign)], vx_s.at[d], vx_r.at[d], dev_x(-sign))
        piece = part_half(-sign, d)
        pending.append(send(piece, piece, vf_s.at[d], vf_r.at[d], dev_x(sign)))
    local[5].wait()
    land_states(0)
    run(forward_own, 0, PAIRS // 2 - 1)
    land_og(2)
    land_p(3)
    land_z(2, 0)
    send_z(3, 0)
    land_states(1)
    run(forward_other, 0, PAIRS // 2 - 1)
    land_z(2, 1)
    send_z(3, 1)
    for d, sign in SIGNS:
        landed(part_half(2, d), vf_s.at[d], vf_r.at[d], dev_x(-sign))
    run(unpack, 0, NZ - 1)
    run(project, 3)
    run(project, 0)
    local[4].wait()
    landed(og_rows(yl * NCORE + 1 - core), oc_s.at[0], oc_r.at[0], dev_core)
    for d, sign in SIGNS:
        for i in range(3):

            @pl.when(has(-sign * (i + 1)))
            def _():
                piece = og_rows((yl - sign * (i + 1)) * NCORE + 1 - core)
                landed(piece, oc_s.at[1 + 3 * d + i], oc_r.at[1 + 3 * d + i], dev_core)

    run(backward, 0)
    share(3, 0)
    chain(3, near)
    share(0, 0)
    run(backward, 1)
    chain(0, near)
    chain(3, 1 - near)
    land_z(3, 0)
    land_z(3, 1)
    run(project, 1, 2)
    run(backward, 2)
    share(1, 0)
    chain(1, near)
    chain(0, 1 - near)
    run(add_x, 0)
    run(backward, 3)
    share(2, 0)
    chain(2, near)
    chain(1, 1 - near)
    run(add_x, 1)
    chain(2, 1 - near)
    run(add_x, 2)
    run(input_grad, 0, PAIRS - 1)
    run(add_x, 3)
    run(finish_layer, 0, NBLK - 1)
    run(finish_state, 0, NZ // 2 - 1)

    for copy in pending:
        copy.wait_send()
    for d, sign in SIGNS:
        for i in range(3):
            drain_og(i, d, sign)

            @pl.when(has(-sign * (i + 1)))
            def _():
                piece = og_rows((yl - sign * (i + 1)) * NCORE + core)
                sent(piece, piece, oc_s.at[1 + 3 * d + i], oc_r.at[1 + 3 * d + i], dev_core)

    def drain_g(u, carry):
        for j in (1, 2, 3):
            sent(
                g_piece(g_send, j, u), g_piece(g_recv, j, u),
                gx_s.at[j - 1, u], gx_r.at[j - 1, u], dev_x(j),
            )
        two = pl.ds(2 * u, 2)
        sent(gy_send.at[two], gy_recv.at[two], gy_s.at[u], gy_r.at[u], dev_yh)
        return carry

    run(drain_g, 0, NZ // 2 - 1)

    def drain_p(n, carry):
        sent(p_send.at[n], p_recv.at[n], pp_s.at[n], pp_r.at[n], dev_core)
        for d, sign in SIGNS:
            for o in (1, 2, 3):

                @pl.when(has(sign * o))
                def _():
                    sent(
                        r_send.at[d, o - 1, n], r_recv.at[d, o - 1, n],
                        rr_s.at[d, o - 1, n], rr_r.at[d, o - 1, n], dev_yl(sign),
                    )

        return carry

    run(drain_p, 0, NBLK - 1)


def copy_out(*refs):
    ins, outs, held, sems = refs[:3], refs[3:6], refs[6:9], refs[9]
    into, out = [], []
    for i, (a, b, v) in enumerate(zip(ins, outs, held)):
        rows = a.shape[0] // PARTS
        for p in range(PARTS):
            piece = pl.ds(p * rows, rows)
            into.append(pltpu.make_async_copy(a.at[piece], v.at[piece], sems.at[0, i, p]))
            out.append(pltpu.make_async_copy(v.at[piece], b.at[piece], sems.at[1, i, p]))
    for copy in into:
        copy.start()
    for first, second in zip(into, out):
        first.wait()
        second.start()
    for copy in out:
        copy.wait()


def per_device(
    ssm_input,
    b_proj,
    c_proj,
    step_size,
    a_log,
    d_skip,
    out_weight,
    prompt_state,
    prompt_of,
    out_grad,
):
    vmem = pl.BlockSpec(memory_space=pltpu.VMEM)
    anywhere = pl.BlockSpec(memory_space=pl.ANY)
    dma = pltpu.SemaphoreType.DMA
    sems = [
        (2,),
        (2, 3),
        (2, 4, 2),
        (2, 4),
        (2, NZ - 1),
        (2,),
        (2,),
        (),
        (2, 2),
        (2, 2),
        (2, 3),
        (7,),
        (3, NZ // 2),
        (NZ // 2,),
        (NBLK,),
        (2, 3, NBLK),
    ]
    sem_scratch = []
    for shape in sems:
        sem_scratch += [dma(shape), dma(shape)]
    shapes = (
        jax.ShapeDtypeStruct((RESP_ROWS, DW), BF16),
        jax.ShapeDtypeStruct((ROWS, WIDTH), BF16),
        jax.ShapeDtypeStruct((WIDTH, NS), F32),
    )
    results = pl.pallas_call(
        kernel,
        out_shape=shapes,
        in_specs=[pl.BlockSpec(memory_space=pltpu.SMEM)] + [vmem] * 3 + [anywhere] * 6,
        out_specs=(vmem, vmem, vmem),
        scratch_shapes=[
            pltpu.VMEM((ROWS, WIDTH), BF16),
            pltpu.VMEM((ROWS, NS), BF16),
            pltpu.VMEM((ROWS, NS), BF16),
            pltpu.VMEM((ROWS, HEADS), F32),
            pltpu.VMEM((WIDTH, DW), BF16),
            pltpu.VMEM((NX, NZ, NYH, SHARD, DW - CUT), BF16),
            pltpu.VMEM((ROWS, DW), BF16),
            pltpu.VMEM((GROUP, WIDTH, NS), BF16),
            pltpu.VMEM((ROWS, GROUP * NS), BF16),
            pltpu.VMEM((ROWS, WIDTH), F32),
            pltpu.VMEM((ROWS, WIDTH), BF16),
            pltpu.VMEM((ROWS, WIDTH), BF16),
            pltpu.VMEM((ROWS, WIDTH), F32),
            pltpu.VMEM((ROWS, WIDTH), BF16),
            pltpu.VMEM((ROWS, WIDTH), BF16),
            pltpu.VMEM((ROWS, BLK), F32),
            pltpu.VMEM((NBLK, NYL, RESP_ROWS, BLK), BF16),
            pltpu.VMEM((NBLK, NYL, RESP_ROWS, BLK), BF16),
            pltpu.VMEM((NBLK, NYL, RESP_ROWS, BLK), F32),
            pltpu.VMEM((2, 3, NBLK, RESP_ROWS, BLK), BF16),
            pltpu.VMEM((2, 3, NBLK, RESP_ROWS, BLK), BF16),
            pltpu.VMEM((2 * LANE, GROUP * NS), F32),
            pltpu.VMEM((NZ, NYH, LANE, NS), F32),
            pltpu.VMEM((3, NZ, NYH, LANE, NS), BF16),
            pltpu.VMEM((3, NZ, NYH, LANE, NS), BF16),
            pltpu.VMEM((NZ, LANE, NS), BF16),
            pltpu.VMEM((NZ, LANE, NS), BF16),
            dma((7,)),
        ]
        + sem_scratch,
        compiler_params=pltpu.CompilerParams(
            collective_id=0, has_side_effects=True, vmem_limit_bytes=56 * 1024 * 1024
        ),
        name="ssd_span",
    )(
        prompt_of,
        step_size.T,
        a_log.reshape(1, HEADS),
        d_skip.reshape(1, HEADS),
        ssm_input,
        b_proj,
        c_proj,
        out_weight,
        prompt_state.reshape(WIDTH, NS),
        out_grad,
    )
    layer_out, grad_input, grad_state = pl.pallas_call(
        copy_out,
        out_shape=shapes,
        in_specs=[anywhere] * 3,
        out_specs=(anywhere,) * 3,
        scratch_shapes=[pltpu.VMEM(shape.shape, shape.dtype) for shape in shapes]
        + [dma((2, 3, PARTS))],
        compiler_params=pltpu.CompilerParams(vmem_limit_bytes=56 * 1024 * 1024),
        name="hand_out",
    )(*results)
    return layer_out, grad_input, grad_state.reshape(1, HEADS, WIDTH // HEADS, NS)


def solution(mesh):
    placed = (
        P("resp", "head"),
        P("resp", "head"),
        P("resp", "head"),
        P("resp", "head"),
        P("head"),
        P("head"),
        P(("head", "resp"), None),
        P("resp", "head", None, None),
        P("resp"),
        P(("resp", "head"), None),
    )
    return jax.shard_map(
        per_device,
        mesh=mesh,
        in_specs=placed,
        out_specs=(P(("resp", "head"), None), P("resp", "head"), P("resp", "head", None, None)),
        check_vma=False,
    )
```

```python
import functools

import jax
import jax.numpy as jnp
from jax import lax
from jax.experimental import pallas as pl
from jax.experimental.pallas import tpu as pltpu
from jax.sharding import PartitionSpec as P

MESH = pl.DeviceIdType.MESH
F32 = jnp.float32
BF16 = jnp.bfloat16
HIGHEST = lax.Precision.HIGHEST

NX, NYH, NZ, NYL, NCORE = 4, 2, 8, 4, 2
GROUP = NX * NYH
RESP_ROWS = 64
RESPS = 8
ROWS = RESP_ROWS * RESPS
NS = 128
HEADS = 16
WIDTH = 1024
DW = 2048
SHARD = 16
LANE = 128
PAIRS = WIDTH // LANE
PARTS = 2
NBLK = 4
BLK = DW // NBLK
EARLY = BLK
CUT = 1536


def dot_nt(a, b):
    return lax.dot_general(a, b, (((1,), (1,)), ((), ())), preferred_element_type=F32)


def dot_tn(a, b):
    return lax.dot_general(a, b, (((0,), (0,)), ((), ())), preferred_element_type=F32)


def chunk_of(z, s):
    far = (s + 1) // 2
    sign = 1 - 2 * (s % 2)
    return lax.rem(z + NZ + sign * far, NZ)


def kernel(
    prompt_ref,
    step_ref,
    alog_ref,
    skip_ref,
    x_hbm,
    b_hbm,
    c_hbm,
    w_ref,
    state_ref,
    og_ref,
    layer_hbm,
    gin_hbm,
    gstate_hbm,
    layer_ref,
    gin_ref,
    gstate_ref,
    x_ref,
    b_ref,
    c_ref,
    steps_ref,
    w_all,
    w_part,
    og_all,
    states,
    csel,
    inner,
    mix,
    mix_t,
    growth,
    ssm,
    back,
    p_tmp,
    p_send,
    p_recv,
    r_own,
    r_send,
    r_recv,
    g_tmp,
    g_own,
    g_send,
    g_recv,
    gy_send,
    gy_recv,
    loc_sem,
    wy_s,
    wy_r,
    wx_s,
    wx_r,
    wz_s,
    wz_r,
    pz_s,
    pz_r,
    vz_s,
    vz_r,
    vx_s,
    vx_r,
    vf_s,
    vf_r,
    sy_s,
    sy_r,
    sx_s,
    sx_r,
    sf_s,
    sf_r,
    oy_s,
    oy_r,
    oc_s,
    oc_r,
    gx_s,
    gx_r,
    gy_s,
    gy_r,
    pp_s,
    pp_r,
    rr_s,
    rr_r,
):
    resp = lax.axis_index("resp")
    head = lax.axis_index("head")
    x = lax.rem(resp, NX)
    yh = lax.rem(resp // NX, NYH)
    z = resp // GROUP
    core = lax.rem(head, NCORE)
    yl = head // NCORE

    def resp_at(z_, yh_, x_):
        return z_ * GROUP + yh_ * NX + x_

    def x_at(j):
        return lax.rem(x + NX + j, NX)

    def z_at(j):
        return lax.rem(z + NZ + j, NZ)

    def dev_x(j):
        return (resp_at(z, yh, x_at(j)), head)

    def dev_z(j):
        return (resp_at(z_at(j), yh, x), head)

    dev_yh = (resp_at(z, 1 - yh, x), head)
    dev_core = (resp, yl * NCORE + 1 - core)

    def dev_yl(j):
        return (resp, (yl + j) * NCORE + core)

    def send(src, dst, ss, rs, dev):
        copy = pltpu.make_async_remote_copy(
            src_ref=src, dst_ref=dst, send_sem=ss, recv_sem=rs, device_id=dev, device_id_type=MESH
        )
        copy.start()
        return copy

    def landed(dst, ss, rs, dev):
        pltpu.make_async_remote_copy(
            src_ref=dst, dst_ref=dst, send_sem=ss, recv_sem=rs, device_id=dev, device_id_type=MESH
        ).wait_recv()

    def sent(src, dst, ss, rs, dev):
        pltpu.make_async_remote_copy(
            src_ref=src, dst_ref=dst, send_sem=ss, recv_sem=rs, device_id=dev, device_id_type=MESH
        ).wait_send()

    pending = []
    SIGNS = ((0, 1), (1, -1))

    def has(j):
        return yl + j < NYL if j > 0 else yl + j >= 0

    barrier = pltpu.get_barrier_semaphore()
    partners = [dev_yh, dev_core] + [dev_z(j) for j in range(1, NZ)]
    partners += [dev_x(j) for j in range(1, NX)]
    partners += [(resp, lax.rem(yl + j, NYL) * NCORE + core) for j in (1, NYL - 1)]
    for dev in partners:
        pl.semaphore_signal(barrier, inc=1, device_id=dev, device_id_type=MESH)
    local = [
        pltpu.make_async_copy(c_hbm, c_ref, loc_sem.at[0]),
        pltpu.make_async_copy(b_hbm, b_ref, loc_sem.at[1]),
    ]
    for copy in local:
        copy.start()
    pl.semaphore_wait(barrier, len(partners))
    def w_rows(z_, yh_, x_):
        return pl.ds(pl.multiple_of(resp_at(z_, yh_, x_) * SHARD, SHARD), SHARD)

    def w_half(z_, yh_):
        start = (z_ * NYH + yh_) * (NX * SHARD)
        return pl.ds(pl.multiple_of(start, NX * SHARD), NX * SHARD)

    def og_rows(h_):
        return og_all.at[pl.ds(pl.multiple_of(h_ * RESP_ROWS, RESP_ROWS), RESP_ROWS), :]

    w_a, w_b = w_ref.at[:, 0:CUT], w_ref.at[:, CUT:DW]
    own_rows, oth_rows = w_rows(z, yh, x), w_rows(z, 1 - yh, x)
    pending.append(send(w_a, w_all.at[own_rows, 0:CUT], wy_s.at[0], wy_r.at[0], dev_yh))
    pending.append(send(w_b, w_part.at[x, z, yh], wy_s.at[1], wy_r.at[1], dev_yh))
    my_slot = yh * NX + x
    pending.append(send(state_ref, states.at[my_slot], sy_s, sy_r, dev_yh))
    for j in (1, 2, 3):
        pending.append(
            send(w_a, w_all.at[own_rows, 0:CUT], wx_s.at[0, j - 1], wx_r.at[0, j - 1], dev_x(j))
        )

    def send_v(half):
        piece = w_part.at[x, z, yh if half == 0 else 1 - yh]
        for j in range(1, NZ):
            pending.append(
                send(
                    w_b if half == 0 else piece, piece,
                    vz_s.at[half, j - 1], vz_r.at[half, j - 1], dev_z(j),
                )
            )

    def land_v(half):
        for j in range(1, NZ):
            piece = w_part.at[x, z_at(-j), yh if half == 0 else 1 - yh]
            landed(piece, vz_s.at[half, j - 1], vz_r.at[half, j - 1], dev_z(-j))

    send_v(0)

    def send_og(i, d, sign):
        @pl.when(jnp.logical_and(has(sign), has(-sign * i)) if i else has(sign))
        def _():
            piece = og_rows((yl - sign * i) * NCORE + core)
            send(og_ref if i == 0 else piece, piece, oy_s.at[d, i], oy_r.at[d, i], dev_yl(sign))

    def drain_og(i, d, sign):
        @pl.when(jnp.logical_and(has(sign), has(-sign * i)) if i else has(sign))
        def _():
            piece = og_rows((yl - sign * i) * NCORE + core)
            sent(og_ref if i == 0 else piece, piece, oy_s.at[d, i], oy_r.at[d, i], dev_yl(sign))

    def land_og(i):
        for d, sign in SIGNS:

            @pl.when(has(-sign * (i + 1)))
            def _():
                piece = og_rows((yl - sign * (i + 1)) * NCORE + core)
                landed(piece, oy_s.at[d, i], oy_r.at[d, i], dev_yl(-sign))
                send(piece, piece, oc_s.at[1 + 3 * d + i], oc_r.at[1 + 3 * d + i], dev_core)

        if i < 2:
            for d, sign in SIGNS:
                send_og(i + 1, d, sign)

    local += [
        pltpu.make_async_copy(w_a, w_all.at[own_rows, 0:CUT], loc_sem.at[2]),
        pltpu.make_async_copy(w_b, w_part.at[x, z, yh], loc_sem.at[3]),
        pltpu.make_async_copy(og_ref, og_rows(head), loc_sem.at[4]),
        pltpu.make_async_copy(state_ref, states.at[my_slot], loc_sem.at[5]),
        pltpu.make_async_copy(x_hbm, x_ref, loc_sem.at[6]),
    ]
    for copy in local[2:]:
        copy.start()

    base = (resp // GROUP) * GROUP
    steps_ref[...] = jnp.transpose(step_ref[...])

    def fill_csel(r, carry):
        rows = pl.ds(pl.multiple_of(r * RESP_ROWS, RESP_ROWS), RESP_ROWS)
        slot = prompt_ref[r] - base
        c_rows = c_ref[rows, :].astype(F32)
        for k in range(GROUP):
            keep = jnp.where(slot == k, 1.0, 0.0).astype(F32)
            csel[rows, k * NS : (k + 1) * NS] = (c_rows * keep).astype(BF16)
        return carry

    row_id = lax.broadcasted_iota(jnp.int32, (RESP_ROWS, LANE), 0)
    lane_id = lax.broadcasted_iota(jnp.int32, (RESP_ROWS, LANE), 1)
    lane_pos = lax.rem(lane_id, RESP_ROWS)
    first = lane_id < RESP_ROWS
    diag = lane_pos == row_id
    earlier = lane_pos <= row_id
    later = lane_pos >= row_id
    tri = (
        lax.broadcasted_iota(jnp.int32, (RESP_ROWS, RESP_ROWS), 0)
        >= lax.broadcasted_iota(jnp.int32, (RESP_ROWS, RESP_ROWS), 1)
    ).astype(F32)
    a_neg = -jnp.exp(alog_ref[...])

    def spread(columns, i):
        return jnp.where(first, columns[:, 2 * i : 2 * i + 1], columns[:, 2 * i + 1 : 2 * i + 2])

    def fill_mix(r, carry):
        rows = pl.ds(pl.multiple_of(r * RESP_ROWS, RESP_ROWS), RESP_ROWS)
        c_rows, b_rows = c_ref[rows, :], b_ref[rows, :]
        steps = steps_ref[rows, :]
        cum = lax.dot_general(
            tri, steps * a_neg, (((1,), (0,)), ((), ())),
            precision=HIGHEST, preferred_element_type=F32,
        )
        score = dot_nt(c_rows, jnp.concatenate([b_rows, b_rows], axis=0))
        score_t = dot_nt(b_rows, jnp.concatenate([c_rows, c_rows], axis=0))
        for i in range(PAIRS):
            cols = slice(i * LANE, (i + 1) * LANE)
            cum_i, step_i = spread(cum, i), spread(steps, i)
            cum_row = jnp.sum(jnp.where(diag, cum_i, 0.0), axis=0, keepdims=True)
            step_row = jnp.sum(jnp.where(diag, step_i, 0.0), axis=0, keepdims=True)
            differ = cum_i - cum_row
            decay = jnp.exp(jnp.where(earlier, differ, 0.0))
            mix[rows, cols] = jnp.where(earlier, decay * step_row * score, 0.0).astype(BF16)
            decay_t = jnp.exp(jnp.where(later, -differ, 0.0))
            mix_t[rows, cols] = jnp.where(later, decay_t * step_i * score_t, 0.0).astype(BF16)
            growth[rows, cols] = jnp.exp(cum_i)
        return carry

    block_mask = (
        (lax.broadcasted_iota(jnp.int32, (LANE, LANE), 0) < RESP_ROWS)
        == (lax.broadcasted_iota(jnp.int32, (LANE, LANE), 1) < RESP_ROWS)
    ).astype(F32).astype(BF16)

    def blocks_of(pair):
        return jnp.concatenate([pair, pair], axis=0) * block_mask

    def z_pieces(step, half, sent_ones):
        yh_ = yh if half == 0 else 1 - yh
        for d, sign in SIGNS:
            if step == 3 and half != d:
                continue
            z_ = z_at(-sign * (step if sent_ones else step + 1))
            piece = w_all.at[w_half(z_, yh_), EARLY:CUT]
            yield piece, wz_s.at[d, step, half], wz_r.at[d, step, half], sign

    def send_z(step, half):
        for piece, ss, rs, sign in z_pieces(step, half, True):
            pending.append(send(piece, piece, ss, rs, dev_z(sign)))

    def land_z(step, half):
        for piece, ss, rs, sign in z_pieces(step, half, False):
            landed(piece, ss, rs, dev_z(-sign))

    def p_pieces(step, sent_ones):
        for d, sign in SIGNS:
            z_ = z_at(-sign * (step if sent_ones else step + 1))
            if step == 3:
                rows = w_half(z_, yh if d == 0 else 1 - yh)
            else:
                rows = pl.ds(pl.multiple_of(z_ * LANE, LANE), LANE)
            yield w_all.at[rows, 0:EARLY], pz_s.at[d, step], pz_r.at[d, step], sign

    def send_p(step):
        for piece, ss, rs, sign in p_pieces(step, True):
            pending.append(send(piece, piece, ss, rs, dev_z(sign)))

    def land_p(step):
        for piece, ss, rs, sign in p_pieces(step, False):
            landed(piece, ss, rs, dev_z(-sign))

    def slot_of(yh_, j):
        return yh_ * NX + x_at(j)

    def send_states(n):
        yh_ = yh if n == 0 else 1 - yh
        piece = states.at[slot_of(yh_, 0)]
        for d, sign in SIGNS:
            pending.append(
                send(
                    state_ref if n == 0 else piece, piece,
                    sx_s.at[n, d], sx_r.at[n, d], dev_x(sign),
                )
            )

    def pass_states(n):
        yh_ = yh if n == 0 else 1 - yh
        for d, sign in SIGNS:
            landed(states.at[slot_of(yh_, -sign)], sx_s.at[n, d], sx_r.at[n, d], dev_x(-sign))
            piece = states.at[slot_of(yh_, -sign), pl.ds(d * (WIDTH // 2), WIDTH // 2), :]
            pending.append(send(piece, piece, sf_s.at[n, d], sf_r.at[n, d], dev_x(sign)))

    def land_states(n):
        yh_ = yh if n == 0 else 1 - yh
        for d, sign in SIGNS:
            piece = states.at[slot_of(yh_, 2), pl.ds(d * (WIDTH // 2), WIDTH // 2), :]
            landed(piece, sf_s.at[n, d], sf_r.at[n, d], dev_x(-sign))

    def part_half(j, d):
        return w_part.at[x_at(j), pl.ds(d * (NZ // 2), NZ // 2)]

    def spread_row(row_ref, i):
        row = row_ref[...]
        where_first = lax.broadcasted_iota(jnp.int32, (1, LANE), 1) < RESP_ROWS
        out = jnp.zeros((1, LANE), F32)
        for h in range(HEADS):
            keep = jnp.where(h // 2 == i, 1.0, 0.0).astype(F32)
            mine = where_first if h % 2 == 0 else jnp.logical_not(where_first)
            out = out + jnp.where(mine, row[:, h : h + 1] * keep, 0.0)
        return out

    def forward_within(i, carry):
        cols = pl.ds(pl.multiple_of(i * LANE, LANE), LANE)
        skip = spread_row(skip_ref, i)
        for r in range(RESPS):
            rows = slice(r * RESP_ROWS, (r + 1) * RESP_ROWS)
            x_rows = x_ref[rows, cols]
            within = jnp.dot(
                mix[rows, cols], blocks_of(x_rows), preferred_element_type=F32
            )
            inner[rows, cols] = within + skip * x_rows.astype(F32)
        return carry

    def carried(i, yh_):
        cols = pl.ds(pl.multiple_of(i * (2 * LANE), 2 * LANE), 2 * LANE)
        init = jnp.concatenate([states[yh_ * NX + k, cols, :] for k in range(NX)], axis=1)
        mine = csel[:, pl.ds(pl.multiple_of(yh_ * (NX * NS), NX * NS), NX * NS)]
        return cols, dot_nt(mine, init) * growth[:, cols]

    def forward_own(i, carry):
        cols, more = carried(i, yh)
        inner[:, cols] = inner[:, cols] + more
        return carry

    def forward_other(i, carry):
        cols, more = carried(i, 1 - yh)
        ssm[:, cols] = (inner[:, cols] + more).astype(BF16)
        return carry

    def g_piece(ref, j, u):
        return ref.at[j - 1, pl.ds(2 * u, 2)]

    def unpack(z_, carry):
        for yh_ in range(NYH):
            for x_ in range(NX):
                w_all[w_rows(z_, yh_, x_), CUT:DW] = w_part[x_, z_, yh_]
        return carry

    def span_of(s_):
        return pl.ds(pl.multiple_of(chunk_of(z, s_) * LANE, LANE), LANE)

    def backward(u, carry):
        spans = [span_of(2 * u + i) for i in range(2)]
        rows = jnp.concatenate([w_all[span, :] for span in spans], axis=0)
        back_f = dot_nt(og_all[...], rows)
        back_b = back_f.astype(BF16)
        for i in range(2):
            back[:, spans[i]] = back_b[:, i * LANE : (i + 1) * LANE]
        grown = jnp.concatenate([growth[:, span] for span in spans], axis=1)
        scaled = (grown * back_b.astype(F32)).astype(BF16)
        g_tmp[...] = dot_tn(scaled, csel[...])
        for j in range(NX):
            for y in range(NYH):
                k = y * NX + lax.rem(x + j, NX)
                for i in range(2):
                    piece = g_tmp[
                        i * LANE : (i + 1) * LANE, pl.ds(pl.multiple_of(k * NS, NS), NS)
                    ]
                    if j == 0:
                        g_own[2 * u + i, y] = piece
                    else:
                        g_send[j - 1, 2 * u + i, y] = piece.astype(BF16)
            if j > 0:
                send(
                    g_piece(g_send, j, u), g_piece(g_recv, j, u),
                    gx_s.at[j - 1, u], gx_r.at[j - 1, u], dev_x(j),
                )
        return carry

    def add_x(u, carry):
        for j in (1, 2, 3):
            landed(g_piece(g_recv, j, u), gx_s.at[j - 1, u], gx_r.at[j - 1, u], dev_x(-j))

        def total(s_, y):
            return g_own[s_, y] + (
                g_recv[0, s_, y].astype(F32)
                + g_recv[1, s_, y].astype(F32)
                + g_recv[2, s_, y].astype(F32)
            )

        for i in range(2):
            gy_send[2 * u + i] = total(2 * u + i, 1 - yh).astype(BF16)
        two = pl.ds(2 * u, 2)
        send(gy_send.at[two], gy_recv.at[two], gy_s.at[u], gy_r.at[u], dev_yh)
        for i in range(2):
            gstate_ref[span_of(2 * u + i), :] = total(2 * u + i, yh)
        return carry

    def give(n):
        for j in range(NYL):
            p_send[n, j] = p_tmp[
                pl.ds(pl.multiple_of((j * NCORE + 1 - core) * RESP_ROWS, RESP_ROWS), RESP_ROWS), :
            ].astype(BF16)
            r_own[n, j] = p_tmp[
                pl.ds(pl.multiple_of((j * NCORE + core) * RESP_ROWS, RESP_ROWS), RESP_ROWS), :
            ]
        send(p_send.at[n], p_recv.at[n], pp_s.at[n], pp_r.at[n], dev_core)

    def project(n, carry):
        cols = pl.ds(pl.multiple_of(n * BLK, BLK), BLK)
        p_tmp[...] = jnp.dot(ssm[...], w_all[:, cols], preferred_element_type=F32)
        give(n)
        return carry

    def share(n, carry):
        landed(p_recv.at[n], pp_s.at[n], pp_r.at[n], dev_core)
        for j in range(NYL):
            r_own[n, j] = r_own[n, j] + p_recv[n, j].astype(F32)
        return carry

    def chain(n, d):
        sign = 1 - 2 * d

        def here(place):
            return jnp.logical_and(place >= 0, place < NYL)

        for o in (3, 2, 1):

            @pl.when(here(yl + sign * o))
            def _():
                total = r_own[n, yl + sign * o]
                r_send[d, o - 1, n] = total.astype(BF16)
                if o < 3:

                    @pl.when(here(yl - sign))
                    def _():
                        landed(
                            r_recv.at[d, o, n], rr_s.at[d, o, n], rr_r.at[d, o, n], dev_yl(-sign)
                        )
                        r_send[d, o - 1, n] = (total + r_recv[d, o, n].astype(F32)).astype(BF16)

                send(
                    r_send.at[d, o - 1, n], r_recv.at[d, o - 1, n],
                    rr_s.at[d, o - 1, n], rr_r.at[d, o - 1, n], dev_yl(sign),
                )

    def finish_layer(n, carry):
        for d, sign in SIGNS:

            @pl.when(has(-sign))
            def _():
                landed(r_recv.at[d, 0, n], rr_s.at[d, 0, n], rr_r.at[d, 0, n], dev_yl(-sign))
                r_own[n, yl] = r_own[n, yl] + r_recv[d, 0, n].astype(F32)

        layer_ref[:, pl.ds(pl.multiple_of(n * BLK, BLK), BLK)] = r_own[n, yl].astype(BF16)
        return carry

    def input_grad(i, carry):
        cols = pl.ds(pl.multiple_of(i * LANE, LANE), LANE)
        skip = spread_row(skip_ref, i)
        for r in range(RESPS):
            rows = slice(r * RESP_ROWS, (r + 1) * RESP_ROWS)
            b_rows = back[rows, cols]
            within = jnp.dot(
                mix_t[rows, cols], blocks_of(b_rows), preferred_element_type=F32
            )
            gin_ref[rows, cols] = (within + skip * b_rows.astype(F32)).astype(BF16)
        return carry

    def finish_state(u, carry):
        two = pl.ds(2 * u, 2)
        landed(gy_recv.at[two], gy_s.at[u], gy_r.at[u], dev_yh)
        for i in range(2):
            span = span_of(2 * u + i)
            gstate_ref[span, :] = gstate_ref[span, :] + gy_recv[2 * u + i].astype(F32)
        return carry

    def run(body, *indices):
        lax.fori_loop(indices[0], indices[-1] + 1, body, 0)

    near = yl // (NYL // 2)

    local[0].wait()
    local[1].wait()
    run(fill_mix, 0, 2)
    landed(w_all.at[oth_rows, 0:CUT], wy_s.at[0], wy_r.at[0], dev_yh)
    for j in (1, 2, 3):
        piece = w_all.at[oth_rows, 0:CUT]
        pending.append(send(piece, piece, wx_s.at[1, j - 1], wx_r.at[1, j - 1], dev_x(j)))
    landed(w_part.at[x, z, 1 - yh], wy_s.at[1], wy_r.at[1], dev_yh)
    send_v(1)
    send_states(0)
    for d, sign in SIGNS:
        send_og(0, d, sign)
    pending.append(send(og_ref, og_rows(head), oc_s.at[0], oc_r.at[0], dev_core))
    run(fill_mix, 3, 4)
    local[2].wait()
    for n, yh_ in enumerate((yh, 1 - yh)):
        for j in (1, 2, 3):
            piece = w_all.at[w_rows(z, yh_, x_at(-j)), 0:CUT]
            landed(piece, wx_s.at[n, j - 1], wx_r.at[n, j - 1], dev_x(-j))
    send_p(0)
    send_z(0, 0)

    run(fill_csel, 0, RESPS - 1)
    run(fill_mix, 5, 6)
    land_p(0)
    send_p(1)
    send_z(0, 1)
    run(fill_mix, 7)
    land_og(0)
    landed(states.at[slot_of(1 - yh, 0)], sy_s, sy_r, dev_yh)
    send_states(1)
    land_p(1)
    send_p(2)
    land_z(0, 0)
    send_z(1, 0)
    local[3].wait()
    land_v(0)
    land_v(1)
    for d, sign in SIGNS:
        piece = w_part.at[x]
        pending.append(send(piece, piece, vx_s.at[d], vx_r.at[d], dev_x(sign)))
    local[6].wait()
    run(forward_within, 0, 3)
    land_z(0, 1)
    send_z(1, 1)
    pass_states(0)
    land_og(1)
    land_p(2)
    send_p(3)
    land_z(1, 0)
    send_z(2, 0)
    run(forward_within, 4, 7)
    pass_states(1)
    land_z(1, 1)
    send_z(2, 1)
    for d, sign in SIGNS:
        landed(w_part.at[x_at(-sign)], vx_s.at[d], vx_r.at[d], dev_x(-sign))
        piece = part_half(-sign, d)
        pending.append(send(piece, piece, vf_s.at[d], vf_r.at[d], dev_x(sign)))
    local[5].wait()
    land_states(0)
    run(forward_own, 0, PAIRS // 2 - 1)
    land_og(2)
    land_p(3)
    land_z(2, 0)
    send_z(3, 0)
    land_states(1)
    run(forward_other, 0, PAIRS // 2 - 1)
    land_z(2, 1)
    send_z(3, 1)
    for d, sign in SIGNS:
        landed(part_half(2, d), vf_s.at[d], vf_r.at[d], dev_x(-sign))
    run(unpack, 0, NZ - 1)
    run(project, 3)
    run(project, 0)
    local[4].wait()
    landed(og_rows(yl * NCORE + 1 - core), oc_s.at[0], oc_r.at[0], dev_core)
    for d, sign in SIGNS:
        for i in range(3):

            @pl.when(has(-sign * (i + 1)))
            def _():
                piece = og_rows((yl - sign * (i + 1)) * NCORE + 1 - core)
                landed(piece, oc_s.at[1 + 3 * d + i], oc_r.at[1 + 3 * d + i], dev_core)

    run(backward, 0)
    share(3, 0)
    chain(3, near)
    share(0, 0)
    run(backward, 1)
    chain(0, near)
    chain(3, 1 - near)
    land_z(3, 0)
    land_z(3, 1)
    run(project, 1, 2)
    run(backward, 2)
    share(1, 0)
    chain(1, near)
    chain(0, 1 - near)
    run(add_x, 0)
    run(backward, 3)
    share(2, 0)
    chain(2, near)
    chain(1, 1 - near)
    run(add_x, 1)
    chain(2, 1 - near)
    run(add_x, 2)
    results = [
        pltpu.make_async_copy(gin_ref, gin_hbm, loc_sem.at[7]),
        pltpu.make_async_copy(layer_ref, layer_hbm, loc_sem.at[8]),
        pltpu.make_async_copy(gstate_ref, gstate_hbm, loc_sem.at[9]),
    ]
    run(input_grad, 0, PAIRS - 1)
    results[0].start()
    run(add_x, 3)
    run(finish_layer, 0, NBLK - 1)
    results[1].start()
    run(finish_state, 0, NZ // 2 - 1)
    results[2].start()

    for copy in pending:
        copy.wait_send()
    for d, sign in SIGNS:
        for i in range(3):
            drain_og(i, d, sign)

            @pl.when(has(-sign * (i + 1)))
            def _():
                piece = og_rows((yl - sign * (i + 1)) * NCORE + core)
                sent(piece, piece, oc_s.at[1 + 3 * d + i], oc_r.at[1 + 3 * d + i], dev_core)

    def drain_g(u, carry):
        for j in (1, 2, 3):
            sent(
                g_piece(g_send, j, u), g_piece(g_recv, j, u),
                gx_s.at[j - 1, u], gx_r.at[j - 1, u], dev_x(j),
            )
        two = pl.ds(2 * u, 2)
        sent(gy_send.at[two], gy_recv.at[two], gy_s.at[u], gy_r.at[u], dev_yh)
        return carry

    run(drain_g, 0, NZ // 2 - 1)

    def drain_p(n, carry):
        sent(p_send.at[n], p_recv.at[n], pp_s.at[n], pp_r.at[n], dev_core)
        for d, sign in SIGNS:
            for o in (1, 2, 3):

                @pl.when(has(sign * o))
                def _():
                    sent(
                        r_send.at[d, o - 1, n], r_recv.at[d, o - 1, n],
                        rr_s.at[d, o - 1, n], rr_r.at[d, o - 1, n], dev_yl(sign),
                    )

        return carry

    run(drain_p, 0, NBLK - 1)
    for copy in results:
        copy.wait()


def copy_out(*refs):
    ins, outs, held, sems = refs[:3], refs[3:6], refs[6:9], refs[9]
    into, out = [], []
    for i, (a, b, v) in enumerate(zip(ins, outs, held)):
        rows = a.shape[0] // PARTS
        for p in range(PARTS):
            piece = pl.ds(p * rows, rows)
            into.append(pltpu.make_async_copy(a.at[piece], v.at[piece], sems.at[0, i, p]))
            out.append(pltpu.make_async_copy(v.at[piece], b.at[piece], sems.at[1, i, p]))
    for copy in into:
        copy.start()
    for first, second in zip(into, out):
        first.wait()
        second.start()
    for copy in out:
        copy.wait()


def per_device(
    ssm_input,
    b_proj,
    c_proj,
    step_size,
    a_log,
    d_skip,
    out_weight,
    prompt_state,
    prompt_of,
    out_grad,
):
    vmem = pl.BlockSpec(memory_space=pltpu.VMEM)
    anywhere = pl.BlockSpec(memory_space=pl.ANY)
    dma = pltpu.SemaphoreType.DMA
    sems = [
        (2,),
        (2, 3),
        (2, 4, 2),
        (2, 4),
        (2, NZ - 1),
        (2,),
        (2,),
        (),
        (2, 2),
        (2, 2),
        (2, 3),
        (7,),
        (3, NZ // 2),
        (NZ // 2,),
        (NBLK,),
        (2, 3, NBLK),
    ]
    sem_scratch = []
    for shape in sems:
        sem_scratch += [dma(shape), dma(shape)]
    shapes = (
        jax.ShapeDtypeStruct((RESP_ROWS, DW), BF16),
        jax.ShapeDtypeStruct((ROWS, WIDTH), BF16),
        jax.ShapeDtypeStruct((WIDTH, NS), F32),
    )
    results = pl.pallas_call(
        kernel,
        out_shape=shapes,
        in_specs=[pl.BlockSpec(memory_space=pltpu.SMEM)] + [vmem] * 3 + [anywhere] * 6,
        out_specs=(anywhere,) * 3,
        scratch_shapes=[
            pltpu.VMEM((RESP_ROWS, DW), BF16),
            pltpu.VMEM((ROWS, WIDTH), BF16),
            pltpu.VMEM((WIDTH, NS), F32),
            pltpu.VMEM((ROWS, WIDTH), BF16),
            pltpu.VMEM((ROWS, NS), BF16),
            pltpu.VMEM((ROWS, NS), BF16),
            pltpu.VMEM((ROWS, HEADS), F32),
            pltpu.VMEM((WIDTH, DW), BF16),
            pltpu.VMEM((NX, NZ, NYH, SHARD, DW - CUT), BF16),
            pltpu.VMEM((ROWS, DW), BF16),
            pltpu.VMEM((GROUP, WIDTH, NS), BF16),
            pltpu.VMEM((ROWS, GROUP * NS), BF16),
            pltpu.VMEM((ROWS, WIDTH), F32),
            pltpu.VMEM((ROWS, WIDTH), BF16),
            pltpu.VMEM((ROWS, WIDTH), BF16),
            pltpu.VMEM((ROWS, WIDTH), F32),
            pltpu.VMEM((ROWS, WIDTH), BF16),
            pltpu.VMEM((ROWS, WIDTH), BF16),
            pltpu.VMEM((ROWS, BLK), F32),
            pltpu.VMEM((NBLK, NYL, RESP_ROWS, BLK), BF16),
            pltpu.VMEM((NBLK, NYL, RESP_ROWS, BLK), BF16),
            pltpu.VMEM((NBLK, NYL, RESP_ROWS, BLK), F32),
            pltpu.VMEM((2, 3, NBLK, RESP_ROWS, BLK), BF16),
            pltpu.VMEM((2, 3, NBLK, RESP_ROWS, BLK), BF16),
            pltpu.VMEM((2 * LANE, GROUP * NS), F32),
            pltpu.VMEM((NZ, NYH, LANE, NS), F32),
            pltpu.VMEM((3, NZ, NYH, LANE, NS), BF16),
            pltpu.VMEM((3, NZ, NYH, LANE, NS), BF16),
            pltpu.VMEM((NZ, LANE, NS), BF16),
            pltpu.VMEM((NZ, LANE, NS), BF16),
            dma((10,)),
        ]
        + sem_scratch,
        compiler_params=pltpu.CompilerParams(
            collective_id=0, has_side_effects=True, vmem_limit_bytes=56 * 1024 * 1024
        ),
        name="ssd_span",
    )(
        prompt_of,
        step_size.T,
        a_log.reshape(1, HEADS),
        d_skip.reshape(1, HEADS),
        ssm_input,
        b_proj,
        c_proj,
        out_weight,
        prompt_state.reshape(WIDTH, NS),
        out_grad,
    )
    layer_out, grad_input, grad_state = pl.pallas_call(
        copy_out,
        out_shape=shapes,
        in_specs=[anywhere] * 3,
        out_specs=(anywhere,) * 3,
        scratch_shapes=[pltpu.VMEM(shape.shape, shape.dtype) for shape in shapes]
        + [dma((2, 3, PARTS))],
        compiler_params=pltpu.CompilerParams(vmem_limit_bytes=56 * 1024 * 1024),
        name="hand_out",
    )(*results)
    return layer_out, grad_input, grad_state.reshape(1, HEADS, WIDTH // HEADS, NS)


def solution(mesh):
    placed = (
        P("resp", "head"),
        P("resp", "head"),
        P("resp", "head"),
        P("resp", "head"),
        P("head"),
        P("head"),
        P(("head", "resp"), None),
        P("resp", "head", None, None),
        P("resp"),
        P(("resp", "head"), None),
    )
    return jax.shard_map(
        per_device,
        mesh=mesh,
        in_specs=placed,
        out_specs=(P(("resp", "head"), None), P("resp", "head"), P("resp", "head", None, None)),
        check_vma=False,
    )
```
